512 devices in a mesh: outer: 16 (over z), inner: 32 (over x, y, core).
Axes of the slice: x: 4, y: 4, z: 16, core: 2. Of those that a mesh axis runs over, the one named last changes fastest.
Arguments:
- queries_first: bfloat16 [8192, 32, 256], P('inner', 'outer'), may hold values from -80 to 80
- queries_second: bfloat16 [8192, 32, 256], P('inner', 'outer'), may hold values from -80 to 80
- shared_keys: bfloat16 [8192, 256], P(('inner', 'outer')), may hold values from -5 to 5
- shared_values: bfloat16 [8192, 256], P(('inner', 'outer')), may hold values from -6 to 6
Outputs:
- out_first: bfloat16 [8192, 32, 256], P('inner', 'outer')
- out_second: bfloat16 [8192, 32, 256], P('inner', 'outer')
The draws below stay inside these ranges and needn't reach their ends.
All inputs are finite; a program needn't handle non-finite values.
Results may differ from the reference program's by a relative error of at most 0.0035.
Values may be sent and summed in bfloat16 or wider, within the bound.
A program may use at most 128 MiB of HBM per device.

```python
import math
import jax
import jax.numpy as jnp
from jax import lax

H = 32
DH = 256
TOKENS = 8192


def common_base(key):
    return jnp.clip(jax.random.normal(key, (TOKENS, DH), jnp.float32), -5.0, 5.0)


def draw_queries_first(key, part):
    key = jax.random.fold_in(key, 21)
    values = jnp.clip(2.5 * jax.random.normal(key, (TOKENS, H, DH), jnp.float32), -10.0, 10.0)
    return values.astype(jnp.bfloat16)


def draw_queries_second(key, part):
    key = jax.random.fold_in(key, 22)
    values = jnp.clip(2.5 * jax.random.normal(key, (TOKENS, H, DH), jnp.float32), -10.0, 10.0)
    return values.astype(jnp.bfloat16)


def draw_shared_keys(key, part):
    base = common_base(key)
    values = base
    return values.astype(jnp.bfloat16)


def level_of(own_key, dims, pieces, low, top_value):
    gain = 1.0
    for dim, shards_of in pieces:
        heights = jax.random.uniform(jax.random.fold_in(jax.random.fold_in(own_key, 6), dim), (shards_of,), jnp.float32, low / len(pieces), top_value / len(pieces))
        gain = gain * jnp.repeat(jnp.exp(heights), dims[dim] // shards_of).reshape((-1,) + (1,) * (len(dims) - 1 - dim))
    return gain


def bell_draw(stream_key, shape, width, reach, cuts=(), kind=jnp.bfloat16):
    level = level_of(stream_key, shape, cuts, -0.22, 0.18) if cuts else 1.0
    values = jax.random.normal(stream_key, shape, jnp.float32) * width * level
    return jnp.minimum(jnp.maximum(values, -reach), reach).astype(kind)


def setup_inputs(seed: int = 0) -> dict:
    streams_of = jax.random.split(jax.random.key(seed), 5)
    queries_first = draw_queries_first(jax.random.fold_in(streams_of[4], 71), 0)
    queries_second = draw_queries_second(jax.random.fold_in(streams_of[4], 71), 0)
    shared_keys = draw_shared_keys(jax.random.fold_in(streams_of[4], 71), 0)
    shared_values = bell_draw(streams_of[3], (TOKENS, DH), 1.0, 6.0, ((0, 512),))
    return {"queries_first": queries_first, "queries_second": queries_second, "shared_keys": shared_keys, "shared_values": shared_values}


NEGATIVE = -1e+30

def attend(queries, shared_keys, shared_values):
    head_count = queries.shape[1]
    block_rows = math.gcd(TOKENS, 128)
    score_scale = 1.0 / math.sqrt(DH)
    key_pos = jnp.arange(TOKENS, dtype=jnp.int32)

    def one_block(block_index):
        first_row = block_index * block_rows
        query_rows = lax.dynamic_slice_in_dim(queries, first_row, block_rows, 0).reshape(block_rows * head_count, DH)
        scores = jnp.dot(query_rows, shared_keys.T, preferred_element_type=jnp.float32) * score_scale
        positions = first_row + jnp.arange(block_rows * head_count, dtype=jnp.int32) // head_count
        allowed = key_pos[None, :] <= positions[:, None]
        scores = jnp.where(allowed, scores, NEGATIVE)
        row_peak = lax.optimization_barrier(jnp.max(scores, axis=1, keepdims=True))
        weights = jnp.where(allowed, jnp.exp(scores - row_peak), 0.0)
        totals = lax.optimization_barrier(jnp.sum(weights, axis=1, keepdims=True))
        mixed_out = jnp.dot(weights.astype(jnp.bfloat16), shared_values, preferred_element_type=jnp.float32) / totals
        return mixed_out.reshape(block_rows, head_count, DH).astype(jnp.bfloat16)
    blocks = lax.map(one_block, jnp.arange(TOKENS // block_rows, dtype=jnp.int32))
    return blocks.reshape(TOKENS, head_count, DH)

def reference(queries_first, queries_second, shared_keys, shared_values):
    return (attend(queries_first, shared_keys, shared_values), attend(queries_second, shared_keys, shared_values))
```

```python
import functools
import math

import jax
import jax.numpy as jnp
from jax import lax
from jax.experimental import pallas as pl
from jax.experimental.pallas import tpu as pltpu
from jax.sharding import PartitionSpec as P

MESH = pl.DeviceIdType.MESH
MASKED = -1e30
FLOOR = -1e20
SIDE = 4
DEPTH = 16
SHARD = 16
GROUPS = 8
GROUP_ROWS = 2 * SHARD
BLOCK = DEPTH * SHARD
HALF = SIDE * GROUP_ROWS
LAYER_ROWS = 2 * BLOCK
WIDTH = 256
OFF_OWN, OFF_A1, OFF_A2, OFF_B1, OFF_B2, OFF_USE = 0, 1, 2, 3, 4, 5
TICKS = GROUPS + OFF_USE
TILE = 256


def attention_kernel(
    scale2,
    q1_hbm,
    q2_hbm,
    k_hbm,
    v_hbm,
    o1_ref,
    o2_ref,
    kv,
    q_in,
    q_rows,
    row_max,
    row_sum,
    acc,
    in_sem,
    z_send,
    z_recv,
    a_send,
    a_recv,
    b_send,
    b_recv,
    s_send,
    s_recv,
):
    z = lax.axis_index("outer")
    place = lax.axis_index("inner")
    core = lax.rem(place, 2)
    chip = place // 2
    x = chip // SIDE
    y = lax.rem(chip, SIDE)
    flip = 1 - core
    a = x * flip + y * core
    b = y * flip + x * core

    def shift(value, by, size):
        return lax.rem(value + by + size, size)

    def inner_of(a_place, b_place):
        x_place = a_place * flip + b_place * core
        y_place = b_place * flip + a_place * core
        return (x_place * SIDE + y_place) * 2 + core

    dev_zp = (shift(z, 1, DEPTH), place)
    dev_zm = (shift(z, -1, DEPTH), place)
    dev_ap = (z, inner_of(shift(a, 1, SIDE), b))
    dev_am = (z, inner_of(shift(a, -1, SIDE), b))
    dev_bp = (z, inner_of(a, shift(b, 1, SIDE)))
    dev_bm = (z, inner_of(a, shift(b, -1, SIDE)))
    dev_sib = (z, place + 1 - 2 * core)
    am, ap = shift(a, -1, SIDE), shift(a, 1, SIDE)
    bm, bp, bo = shift(b, -1, SIDE), shift(b, 1, SIDE), shift(b, 2, SIDE)

    first_copies = [
        pltpu.make_async_copy(k_hbm, kv.at[core, 0, b, a, 0, pl.ds(0, SHARD)], in_sem.at[0]),
        pltpu.make_async_copy(v_hbm, kv.at[core, 0, b, a, 1, pl.ds(0, SHARD)], in_sem.at[1]),
    ]
    q_copies = [
        pltpu.make_async_copy(source, q_in.at[n], in_sem.at[2 + n])
        for n, source in enumerate((q1_hbm, q2_hbm))
    ]
    for copy in first_copies + q_copies:
        copy.start()

    barrier = pltpu.get_barrier_semaphore()
    for device in (dev_zp, dev_zm, dev_ap, dev_am, dev_bp, dev_bm, dev_sib):
        pl.semaphore_signal(barrier, inc=1, device_id=device, device_id_type=MESH)
    for copy in first_copies:
        copy.wait()
    pl.semaphore_wait(barrier, 7)

    def remote(src, dst, send, recv, device):
        return pltpu.make_async_remote_copy(
            src_ref=src,
            dst_ref=dst,
            send_sem=send,
            recv_sem=recv,
            device_id=device,
            device_id_type=MESH,
        )

    def shard(g, half):
        return kv.at[core, g, b, a, :, pl.ds(half * SHARD, SHARD)]

    def z_up(s, first=False):
        source = shard(0, 0) if first else shard(jnp.maximum(s - 2, 0), 1)
        return remote(source, shard(s - 1, 1), z_send.at[0, s - 1], z_recv.at[0, s - 1], dev_zm)

    def z_down(s):
        return remote(shard(s - 1, 0), shard(s, 0), z_send.at[1, s - 1], z_recv.at[1, s - 1], dev_zp)

    def own(g, way):
        piece = kv.at[core, g, b, a]
        return remote(piece, piece, a_send.at[way, g], a_recv.at[way, g], (dev_ap, dev_am)[way])

    def a_on(g, way):
        piece = kv.at[core, g, b, (am, ap)[way], way]
        return remote(piece, piece, a_send.at[2 + way, g], a_recv.at[2 + way, g], (dev_ap, dev_am)[way])

    def row_out(g, way):
        piece = kv.at[core, g, b]
        return remote(piece, piece, b_send.at[way, g], b_recv.at[way, g], (dev_bp, dev_bm)[way])

    def b_on(g, way):
        piece = kv.at[core, g, (bm, bp)[way], :, way]
        return remote(piece, piece, b_send.at[2 + way, g], b_recv.at[2 + way, g], (dev_bp, dev_bm)[way])

    def across(g, which):
        piece = kv.at[core, g, (b, bm, bp, bo)[which]]
        return remote(piece, piece, s_send.at[which, g], s_recv.at[which, g], dev_sib)

    z_up(1, True).start()
    z_down(1).start()

    def stage_own(g):
        z_up(g + 1).wait_recv()

        @pl.when(g < GROUPS - 1)
        def _():
            z_up(g + 2).start()
            own(g, 0).start()
            own(g, 1).start()
            z_down(g + 1).wait_recv()

        @pl.when(g == GROUPS - 1)
        def _():
            own(g, 0).start()
            own(g, 1).start()

        @pl.when(g < GROUPS - 2)
        def _():
            z_down(g + 2).start()

    def stage_a1(g):
        for way in (0, 1):
            own(g, way).wait_recv()
            a_on(g, way).start()

    def stage_a2(g):
        for way in (0, 1):
            a_on(g, way).wait_recv()
        for way in (0, 1):
            row_out(g, way).start()
        across(g, 0).start()

    def stage_b1(g):
        for way in (0, 1):
            row_out(g, way).wait_recv()
            b_on(g, way).start()
            across(g, 1 + way).start()

    def stage_b2(g):
        for way in (0, 1):
            b_on(g, way).wait_recv()
        across(g, 3).start()

    def prepare():
        row_max[...] = jnp.full_like(row_max, FLOOR)
        row_sum[...] = jnp.zeros_like(row_sum)
        acc[...] = jnp.zeros_like(acc)
        for n, copy in enumerate(q_copies):
            copy.wait()
            q_rows[n * LAYER_ROWS : (n + 1) * LAYER_ROWS] = q_in[n].reshape(LAYER_ROWS, WIDTH)

    def attend(g, layer, last):
        def keys_of(which):
            pieces = []
            for x_key in range(last + 1):
                pieces.append(kv[0, g, :, x_key, which].reshape(HALF, WIDTH))
                pieces.append(kv[1, g, x_key, :, which].reshape(HALF, WIDTH))
            return jnp.concatenate(pieces, axis=0)

        keys = keys_of(0)
        values = keys_of(1)
        at = lax.broadcasted_iota(jnp.int32, (1, 2 * HALF), 1)
        from_core = at // HALF
        y_key = lax.rem(at // GROUP_ROWS, SIDE)
        z_rel = jnp.where(lax.rem(at // SHARD, 2) == 0, -g, g + 1)
        z_key = lax.rem(z + z_rel + DEPTH, DEPTH)
        key_pos = ((last * SIDE + y_key) * 2 + from_core) * BLOCK + z_key * SHARD + lax.rem(at, SHARD)
        open_width = 2 * HALF * last
        lanes = 2 * (last + 1)
        for tile in range(LAYER_ROWS // TILE):
            here = pl.ds(layer * LAYER_ROWS + tile * TILE, TILE)
            scores = lax.dot_general(
                q_rows[here], keys, (((1,), (1,)), ((), ())), preferred_element_type=jnp.float32
            )
            row = lax.broadcasted_iota(jnp.int32, (TILE, 1), 0) + tile * TILE
            allowed = key_pos <= place * BLOCK + row // 2
            edge = jnp.where(allowed, scores[:, open_width:], MASKED)
            pieces = [scores[:, n * 128 : (n + 1) * 128] for n in range(lanes - 2)]
            pieces += [edge[:, :128], edge[:, 128:]]
            peak = functools.reduce(jnp.maximum, pieces)
            old = row_max[here]
            new = jnp.maximum(old, jnp.max(peak, axis=1, keepdims=True))
            fade = jnp.exp2((old - new) * scale2)
            weights = [jnp.exp2((piece - new) * scale2) for piece in pieces]
            row_max[here] = new
            row_sum[here] = row_sum[here] * fade + functools.reduce(jnp.add, weights)
            rounded = jnp.concatenate([w.astype(jnp.bfloat16) for w in weights], axis=1)
            mixed = jnp.dot(rounded, values, preferred_element_type=jnp.float32)
            acc[here] = acc[here] * jnp.concatenate((fade, fade), axis=1) + mixed

    def use(g, layer):
        for last in range(SIDE):

            @pl.when(x == last)
            def _(last=last):
                attend(g, layer, last)

    def stage_use(g):
        for which in range(4):
            across(g, which).wait_recv()
        use(g, 0)

    def stage_use_second(g):
        use(g, 1)

    def drain(g):
        z_up(g + 1).wait_send()

        @pl.when(g < GROUPS - 1)
        def _():
            z_down(g + 1).wait_send()

        for way in (0, 1):
            own(g, way).wait_send()
            a_on(g, way).wait_send()
            row_out(g, way).wait_send()
            b_on(g, way).wait_send()
        for which in range(4):
            across(g, which).wait_send()

    stages = (
        (OFF_OWN, stage_own),
        (OFF_A1, stage_a1),
        (OFF_A2, stage_a2),
        (OFF_USE, stage_use),
        (OFF_B1, stage_b1),
        (OFF_B2, stage_b2),
        (OFF_USE, stage_use_second),
    )

    @pl.loop(0, TICKS)
    def _(tick):
        for offset, stage in stages:
            g = tick - offset

            @pl.when((g >= 0) & (g < GROUPS))
            def _(stage=stage, g=g):
                stage(g)

        @pl.when(tick == 1)
        def _():
            prepare()

    @pl.loop(0, GROUPS)
    def _(g):
        drain(g)

    for layer, o_ref in enumerate((o1_ref, o2_ref)):
        for part in range(LAYER_ROWS // TILE):
            here = pl.ds(layer * LAYER_ROWS + part * TILE, TILE)
            inverse = 1.0 / jnp.sum(row_sum[here], axis=1, keepdims=True)
            o_ref[part * TILE : (part + 1) * TILE] = (acc[here] * inverse).astype(jnp.bfloat16)


def on_device(queries_first, queries_second, shared_keys, shared_values):
    tokens_here, heads, width = queries_first.shape
    rows = 2 * tokens_here * heads
    scale2 = math.log2(math.e) / math.sqrt(width)
    dma = pltpu.SemaphoreType.DMA
    out = jax.ShapeDtypeStruct((rows // 2, width), jnp.bfloat16)
    vmem = pl.BlockSpec(memory_space=pltpu.VMEM)
    result = pl.pallas_call(
        functools.partial(attention_kernel, scale2),
        out_shape=(out, out),
        in_specs=[pl.BlockSpec(memory_space=pl.ANY)] * 4,
        out_specs=(vmem, vmem),
        scratch_shapes=[
            pltpu.VMEM((2, GROUPS, SIDE, SIDE, 2, GROUP_ROWS, width), jnp.bfloat16),
            pltpu.VMEM((2, tokens_here, heads, width), jnp.bfloat16),
            pltpu.VMEM((rows, width), jnp.bfloat16),
            pltpu.VMEM((rows, 128), jnp.float32),
            pltpu.VMEM((rows, 128), jnp.float32),
            pltpu.VMEM((rows, width), jnp.float32),
            dma((4,)),
            dma((2, GROUPS)),
            dma((2, GROUPS)),
            dma((4, GROUPS)),
            dma((4, GROUPS)),
            dma((4, GROUPS)),
            dma((4, GROUPS)),
            dma((4, GROUPS)),
            dma((4, GROUPS)),
        ],
        compiler_params=pltpu.CompilerParams(
            collective_id=0, has_side_effects=True, vmem_limit_bytes=56 * 1024 * 1024
        ),
        cost_estimate=pl.CostEstimate(
            flops=4 * rows * 8192 * width, bytes_accessed=1 << 20, transcendentals=rows * 8192
        ),
    )(queries_first, queries_second, shared_keys, shared_values)
    return tuple(array.reshape(tokens_here, heads, width) for array in result)


def solution(mesh):
    return jax.shard_map(
        on_device,
        mesh=mesh,
        in_specs=(
            P("inner", "outer", None),
            P("inner", "outer", None),
            P(("inner", "outer"), None),
            P(("inner", "outer"), None),
        ),
        out_specs=(P("inner", "outer", None), P("inner", "outer", None)),
        check_vma=False,
    )
```

```python
import functools
import math

import jax
import jax.numpy as jnp
from jax import lax
from jax.experimental import pallas as pl
from jax.experimental.pallas import tpu as pltpu
from jax.sharding import PartitionSpec as P

MESH = pl.DeviceIdType.MESH
MASKED = -1e30
FLOOR = -1e20
SIDE = 4
DEPTH = 16
SHARD = 16
GROUP_ROWS = 2 * SHARD
BLOCK = DEPTH * SHARD
HALF = SIDE * GROUP_ROWS
LAYER_ROWS = 2 * BLOCK
ROWS = 2 * LAYER_ROWS
WIDTH = 256
ROUND = ((0, 3), (-3, 1), (5, -5), (7, -7), (-1, 2), (-2, 8))
HOPPED = ((4, -4), (6, -6))
RELATIVE = ROUND + HOPPED
GROUPS = len(ROUND)
HOPS = tuple(
    (which, group, half)
    for which in (0, 1)
    for group in range(GROUPS, len(RELATIVE))
    for half in (0, 1)
)
OFF_OWN, OFF_A1, OFF_A2, OFF_B1, OFF_B2 = 0, 1, 2, 3, 4
TICKS = GROUPS + OFF_B2
TILE = 256
TILES = ROWS // TILE
CHUNK = 64


def place_of(relative):
    for group, members in enumerate(RELATIVE):
        for half, member in enumerate(members):
            if member % DEPTH == relative % DEPTH:
                return group, half
    return None


def attention_kernel(
    scale2,
    q1_hbm,
    q2_hbm,
    k_hbm,
    v_hbm,
    o1_ref,
    o2_ref,
    kv,
    q_in,
    q_cols,
    state,
    acc,
    values_t,
    scores_even,
    scores_odd,
    weights_even,
    weights_odd,
    acc_out,
    acc_in,
    state_in,
    in_sem,
    z_send,
    z_recv,
    a_send,
    a_recv,
    b_send,
    b_recv,
    hop_send,
    hop_recv,
    pair_send,
    pair_recv,
):
    z = lax.axis_index("outer")
    place = lax.axis_index("inner")
    core = lax.rem(place, 2)
    chip = place // 2
    x = chip // SIDE
    y = lax.rem(chip, SIDE)
    flip = 1 - core
    a = x * flip + y * core
    b = y * flip + x * core

    def shift(value, by, size):
        return lax.rem(value + by + size, size)

    def inner_of(a_place, b_place):
        x_place = a_place * flip + b_place * core
        y_place = b_place * flip + a_place * core
        return (x_place * SIDE + y_place) * 2 + core

    dev_zp = (shift(z, 1, DEPTH), place)
    dev_zm = (shift(z, -1, DEPTH), place)
    dev_ap = (z, inner_of(shift(a, 1, SIDE), b))
    dev_am = (z, inner_of(shift(a, -1, SIDE), b))
    dev_bp = (z, inner_of(a, shift(b, 1, SIDE)))
    dev_bm = (z, inner_of(a, shift(b, -1, SIDE)))
    dev_sib = (z, place + 1 - 2 * core)
    am, ap = shift(a, -1, SIDE), shift(a, 1, SIDE)
    bm, bp = shift(b, -1, SIDE), shift(b, 1, SIDE)

    first_copies = [
        pltpu.make_async_copy(k_hbm, kv.at[core, 0, b, a, 0, pl.ds(0, SHARD)], in_sem.at[0]),
        pltpu.make_async_copy(v_hbm, kv.at[core, 0, b, a, 1, pl.ds(0, SHARD)], in_sem.at[1]),
    ]
    q_copies = [
        pltpu.make_async_copy(source, q_in.at[n], in_sem.at[2 + n])
        for n, source in enumerate((q1_hbm, q2_hbm))
    ]
    for copy in first_copies + q_copies:
        copy.start()

    far = [member for pair in ROUND for member in pair if member]
    barrier = pltpu.get_barrier_semaphore()
    for device in (dev_ap, dev_am, dev_bp, dev_bm, dev_sib):
        pl.semaphore_signal(barrier, inc=1, device_id=device, device_id_type=MESH)
    for member in far:
        device = (shift(z, -member, DEPTH), place)
        pl.semaphore_signal(barrier, inc=1, device_id=device, device_id_type=MESH)
    for copy in first_copies:
        copy.wait()
    pl.semaphore_wait(barrier, 5 + len(far))

    def remote(src, dst, send, recv, device):
        return pltpu.make_async_remote_copy(
            src_ref=src,
            dst_ref=dst,
            send_sem=send,
            recv_sem=recv,
            device_id=device,
            device_id_type=MESH,
        )

    def shard(g, half):
        return kv.at[core, g, b, a, :, pl.ds(half * SHARD, SHARD)]

    def z_out(g, half, device):
        return remote(shard(0, 0), shard(g, half), z_send.at[g, half], z_recv.at[g, half], device)

    def own(g, way):
        piece = kv.at[core, g, b, a]
        return remote(piece, piece, a_send.at[way, g], a_recv.at[way, g], (dev_ap, dev_am)[way])

    def a_on(g, way):
        piece = kv.at[core, g, b, (am, ap)[way], way]
        return remote(piece, piece, a_send.at[2 + way, g], a_recv.at[2 + way, g], (dev_ap, dev_am)[way])

    def row_out(g, way):
        piece = kv.at[core, g, b]
        return remote(piece, piece, b_send.at[way, g], b_recv.at[way, g], (dev_bp, dev_bm)[way])

    def b_on(g, way):
        piece = kv.at[core, g, (bm, bp)[way], :, way]
        return remote(piece, piece, b_send.at[2 + way, g], b_recv.at[2 + way, g], (dev_bp, dev_bm)[way])

    def hop(n):
        which, group, half = HOPS[n]
        member = RELATIVE[group][half]
        source_group, source_half = place_of(member - 1 if which == 0 else member + 1)
        source = kv.at[core, source_group, :, :, which, pl.ds(source_half * SHARD, SHARD)]
        target = kv.at[core, group, :, :, which, pl.ds(half * SHARD, SHARD)]
        device = dev_zm if which == 0 else dev_zp
        return source_group, remote(source, target, hop_send.at[n], hop_recv.at[n], device)

    mine, theirs = pl.ds(0, TILES), pl.ds(TILES, TILES)
    q_across = remote(q_cols.at[mine], q_cols.at[theirs], pair_send.at[0], pair_recv.at[0], dev_sib)
    acc_across = remote(acc_out, acc_in, pair_send.at[1], pair_recv.at[1], dev_sib)
    state_across = remote(state.at[theirs], state_in, pair_send.at[2], pair_recv.at[2], dev_sib)

    for member in far:
        z_out(*place_of(member), (shift(z, -member, DEPTH), place)).start()

    def prepare(step):
        if step < 2:
            q_copies[step].wait()
            for part in range(TILES // 2):
                tokens = TILE // 2
                rows = q_in[step, part * tokens : (part + 1) * tokens].reshape(TILE, WIDTH)
                q_cols[step * (TILES // 2) + part] = rows.T
            if step == 1:
                q_across.start()
        else:
            start = (step - 2) * TILES
            acc[start : start + TILES] = jnp.zeros((TILES, WIDTH, TILE), jnp.float32)
            state[start : start + TILES, 0:1] = jnp.full((TILES, 1, TILE), FLOOR, jnp.float32)
            state[start : start + TILES, 1:2] = jnp.zeros((TILES, 1, TILE), jnp.float32)

    def stage_own(g):
        @pl.when(g > 0)
        def _():
            z_out(g, 0, dev_zp).wait_recv()

        z_out(g, 1, dev_zp).wait_recv()
        own(g, 0).start()
        own(g, 1).start()

    def stage_a1(g):
        for way in (0, 1):
            own(g, way).wait_recv()
            a_on(g, way).start()

    def stage_a2(g):
        for way in (0, 1):
            a_on(g, way).wait_recv()
        for way in (0, 1):
            row_out(g, way).start()

    def stage_b1(g):
        for way in (0, 1):
            row_out(g, way).wait_recv()
            b_on(g, way).start()

    def stage_b2(g):
        for way in (0, 1):
            b_on(g, way).wait_recv()
        for n in range(len(HOPS)):
            source_group, copy = hop(n)

            @pl.when(g == source_group)
            def _(copy=copy):
                copy.start()

    def select(g, half):
        value = jnp.int32(0)
        for group, members in enumerate(RELATIVE):
            value = jnp.where(g == group, members[half], value)
        return value

    def attend(g, step, token_block, side, last):
        def keys_of(which):
            pieces = []
            for x_key in range(last + 1):
                piece = kv[0, g, :, x_key, which] if side == 0 else kv[1, g, x_key, :, which]
                pieces.append(piece.reshape(HALF, WIDTH))
            return jnp.concatenate(pieces, axis=0)

        open_keys = last * HALF
        all_keys = open_keys + HALF

        @pl.when(step == 0)
        def _():
            values_t[g, :, :all_keys] = keys_of(1).T

        at = lax.broadcasted_iota(jnp.int32, (HALF, 1), 0)
        y_key = at // GROUP_ROWS
        z_rel = jnp.where(lax.rem(at // SHARD, 2) == 0, select(g, 0), select(g, 1))
        z_key = lax.rem(z + z_rel + DEPTH, DEPTH)
        key_pos = ((last * SIDE + y_key) * 2 + side) * BLOCK + z_key * SHARD + lax.rem(at, SHARD)
        limit = token_block * BLOCK + lax.broadcasted_iota(jnp.int32, (1, TILE), 1) // 2

        base = (1 - step) * TILES
        score_refs = (scores_even, scores_odd)
        weight_refs = (weights_even, weights_odd)
        before = state[pl.ds(base, TILES)]
        maxima, totals, fades = [], [], []

        def score_tile(n):
            score_refs[n % 2][:all_keys] = jnp.dot(
                keys_of(0), q_cols[base + n], preferred_element_type=jnp.float32
            )

        def soften_tile(n):
            source, target = score_refs[n % 2], weight_refs[n % 2]
            allowed = key_pos <= limit + (n % 2) * (TILE // 2)

            def chunk(first):
                scores = source[first : first + CHUNK]
                if first >= open_keys:
                    row = first - open_keys
                    scores = jnp.where(allowed[row : row + CHUNK], scores, MASKED)
                return scores

            def fold(op, values):
                return functools.reduce(op, [values[i : i + 8] for i in range(0, CHUNK, 8)])

            peak = functools.reduce(
                jnp.maximum, [fold(jnp.maximum, chunk(first)) for first in range(0, all_keys, CHUNK)]
            )
            old = before[n, 0:1]
            new = jnp.maximum(old, jnp.max(peak, axis=0, keepdims=True))
            total = jnp.zeros((8, TILE), jnp.float32)
            for first in range(0, all_keys, CHUNK):
                weights = jnp.exp2((chunk(first) - new) * scale2)
                total = total + fold(jnp.add, weights)
                target[first : first + CHUNK] = weights.astype(jnp.bfloat16)
            fade = jnp.exp2((old - new) * scale2)
            fades.append(fade)
            maxima.append(new)
            totals.append(before[n, 1:2] * fade + jnp.sum(total, axis=0, keepdims=True))

        def mix_tile(n):
            mixed = jnp.dot(
                values_t[g, :, :all_keys],
                weight_refs[n % 2][:all_keys],
                preferred_element_type=jnp.float32,
            )
            acc[base + n] = acc[base + n] * fades[n] + mixed

        score_tile(0)
        for n in range(TILES):
            if n + 1 < TILES:
                score_tile(n + 1)
            if n:
                mix_tile(n - 1)
            soften_tile(n)
        mix_tile(TILES - 1)
        for n in range(TILES):
            state[base + n, 0:1] = maxima[n]
            state[base + n, 1:2] = totals[n]

    def use(g, step):
        token_block = place + (1 - step) * (1 - 2 * core)
        for side in (0, 1):
            for last in range(SIDE):

                @pl.when((core == side) & (x == last))
                def _(side=side, last=last):
                    attend(g, step, token_block, side, last)

    def hand_over():
        state_across.start()
        for tile in range(TILES):
            acc_out[tile] = acc[TILES + tile].astype(jnp.bfloat16)
        acc_across.start()

    stages = (
        (OFF_OWN, stage_own),
        (OFF_A1, stage_a1),
        (OFF_A2, stage_a2),
        (OFF_B1, stage_b1),
        (OFF_B2, stage_b2),
    )
    hop_tick = OFF_B2 + 3

    @pl.loop(0, TICKS)
    def _(tick):
        for offset, stage in stages:
            g = tick - offset

            @pl.when((g >= 0) & (g < GROUPS))
            def _(stage=stage, g=g):
                stage(g)

        for step in range(OFF_B2):

            @pl.when(tick == step)
            def _(step=step):
                prepare(step)

        @pl.when(tick == OFF_B2)
        def _():
            q_across.wait_recv()

        hopped = (tick >= hop_tick) & (tick < hop_tick + len(HOPPED))
        closing = tick == TICKS - 1
        first = tick - OFF_B2
        hop_group = tick - hop_tick + GROUPS
        count = jnp.where(
            first < 0, 0, jnp.where(hopped, 4, jnp.where(closing, 3, jnp.where(first == 0, 1, 2)))
        )

        @pl.loop(0, count)
        def _(item):
            for n, (_, group, _) in enumerate(HOPS):

                @pl.when((item == 2) & hopped & (hop_group == group))
                def _(n=n):
                    hop(n)[1].wait_recv()

            @pl.when(closing & (item == 1))
            def _():
                hand_over()

            group = jnp.where(
                item == 0, first, jnp.where(item == 1, first - 1, jnp.where(closing, first, hop_group))
            )
            use(group, jnp.where(item == 2, jnp.where(closing, 1, 0), jnp.minimum(item, 1)))

    for member in far:
        z_out(*place_of(member), dev_zp).wait_send()
    for n in range(len(HOPS)):
        hop(n)[1].wait_send()
    q_across.wait_send()

    @pl.loop(0, GROUPS)
    def _(g):
        for way in (0, 1):
            own(g, way).wait_send()
            a_on(g, way).wait_send()
            row_out(g, way).wait_send()
            b_on(g, way).wait_send()

    state_across.wait()
    acc_across.wait()
    for layer, o_ref in enumerate((o1_ref, o2_ref)):
        for part in range(TILES // 2):
            tile = layer * (TILES // 2) + part
            here, there = state[tile, 0:1], state_in[tile, 0:1]
            peak = jnp.maximum(here, there)
            keep = jnp.exp2((here - peak) * scale2)
            add = jnp.exp2((there - peak) * scale2)
            inverse = 1.0 / (state[tile, 1:2] * keep + state_in[tile, 1:2] * add)
            result = acc[tile] * (keep * inverse) + acc_in[tile].astype(jnp.float32) * (add * inverse)
            o_ref[part * TILE : (part + 1) * TILE] = result.T.astype(jnp.bfloat16)


def on_device(queries_first, queries_second, shared_keys, shared_values):
    tokens_here, heads, width = queries_first.shape
    rows = 2 * tokens_here * heads
    scale2 = math.log2(math.e) / math.sqrt(width)
    dma = pltpu.SemaphoreType.DMA
    out = jax.ShapeDtypeStruct((rows // 2, width), jnp.bfloat16)
    vmem = pl.BlockSpec(memory_space=pltpu.VMEM)
    result = pl.pallas_call(
        functools.partial(attention_kernel, scale2),
        out_shape=(out, out),
        in_specs=[pl.BlockSpec(memory_space=pl.ANY)] * 4,
        out_specs=(vmem, vmem),
        scratch_shapes=[
            pltpu.VMEM((2, len(RELATIVE), SIDE, SIDE, 2, GROUP_ROWS, width), jnp.bfloat16),
            pltpu.VMEM((2, tokens_here, heads, width), jnp.bfloat16),
            pltpu.VMEM((2 * TILES, width, TILE), jnp.bfloat16),
            pltpu.VMEM((2 * TILES, 2, TILE), jnp.float32),
            pltpu.VMEM((2 * TILES, width, TILE), jnp.float32),
            pltpu.VMEM((len(RELATIVE), width, SIDE * HALF), jnp.bfloat16),
            pltpu.VMEM((SIDE * HALF, TILE), jnp.float32),
            pltpu.VMEM((SIDE * HALF, TILE), jnp.float32),
            pltpu.VMEM((SIDE * HALF, TILE), jnp.bfloat16),
            pltpu.VMEM((SIDE * HALF, TILE), jnp.bfloat16),
            pltpu.VMEM((TILES, width, TILE), jnp.bfloat16),
            pltpu.VMEM((TILES, width, TILE), jnp.bfloat16),
            pltpu.VMEM((TILES, 2, TILE), jnp.float32),
            dma((4,)),
            dma((GROUPS, 2)),
            dma((GROUPS, 2)),
            dma((4, GROUPS)),
            dma((4, GROUPS)),
            dma((4, GROUPS)),
            dma((4, GROUPS)),
            dma((len(HOPS),)),
            dma((len(HOPS),)),
            dma((3,)),
            dma((3,)),
        ],
        compiler_params=pltpu.CompilerParams(
            collective_id=0, has_side_effects=True, vmem_limit_bytes=56 * 1024 * 1024
        ),
        cost_estimate=pl.CostEstimate(
            flops=4 * rows * 8192 * width, bytes_accessed=1 << 20, transcendentals=rows * 8192
        ),
    )(queries_first, queries_second, shared_keys, shared_values)
    return tuple(array.reshape(tokens_here, heads, width) for array in result)


def solution(mesh):
    return jax.shard_map(
        on_device,
        mesh=mesh,
        in_specs=(
            P("inner", "outer", None),
            P("inner", "outer", None),
            P(("inner", "outer"), None),
            P(("inner", "outer"), None),
        ),
        out_specs=(P("inner", "outer", None), P("inner", "outer", None)),
        check_vma=False,
    )
```

```python
import functools
import math

import jax
import jax.numpy as jnp
from jax import lax
from jax.experimental import pallas as pl
from jax.experimental.pallas import tpu as pltpu
from jax.sharding import PartitionSpec as P

MESH = pl.DeviceIdType.MESH
MASKED = -1e30
FLOOR = -1e20
SIDE = 4
DEPTH = 16
SHARD = 16
GROUP_ROWS = 2 * SHARD
BLOCK = DEPTH * SHARD
HALF = SIDE * GROUP_ROWS
LAYER_ROWS = 2 * BLOCK
WIDTH = 256
ROUND = ((0, 1), (3, -3), (5, -5), (7, -7), (-1, 2), (-2, 8))
HOPPED = ((4, -4), (6, -6))
RELATIVE = ROUND + HOPPED
GROUPS = len(ROUND)
HOPS = tuple(
    (which, group, half)
    for group in range(GROUPS, len(RELATIVE))
    for which in (0, 1)
    for half in (0, 1)
)
ONWARD = ((1, -2, 3), (-1, 2, -3), (3, -2, 5), (-3, 2, -5), (5, -2, 7), (-5, 2, -7), (7, -1, 8))
OFF_OWN, OFF_A1, OFF_A2, OFF_B1, OFF_B2, OFF_USE = 0, 1, 2, 3, 4, 5
TICKS = GROUPS + OFF_USE
TILE = 256


def place_of(relative):
    for group, members in enumerate(RELATIVE):
        for half, member in enumerate(members):
            if member % DEPTH == relative % DEPTH:
                return group, half
    return None


def attention_kernel(
    scale2,
    q1_hbm,
    q2_hbm,
    k_hbm,
    v_hbm,
    o1_ref,
    o2_ref,
    kv,
    q_in,
    q_rows,
    row_max,
    row_sum,
    acc,
    in_sem,
    z_send,
    z_recv,
    a_send,
    a_recv,
    b_send,
    b_recv,
    s_send,
    s_recv,
    hop_send,
    hop_recv,
):
    z = lax.axis_index("outer")
    place = lax.axis_index("inner")
    core = lax.rem(place, 2)
    chip = place // 2
    x = chip // SIDE
    y = lax.rem(chip, SIDE)
    flip = 1 - core
    a = x * flip + y * core
    b = y * flip + x * core

    def shift(value, by, size):
        return lax.rem(value + by + size, size)

    def inner_of(a_place, b_place):
        x_place = a_place * flip + b_place * core
        y_place = b_place * flip + a_place * core
        return (x_place * SIDE + y_place) * 2 + core

    along_z = {by: (shift(z, by, DEPTH), place) for by in (-2, -1, 1, 2)}
    dev_ap = (z, inner_of(shift(a, 1, SIDE), b))
    dev_am = (z, inner_of(shift(a, -1, SIDE), b))
    dev_bp = (z, inner_of(a, shift(b, 1, SIDE)))
    dev_bm = (z, inner_of(a, shift(b, -1, SIDE)))
    dev_sib = (z, place + 1 - 2 * core)
    am, ap = shift(a, -1, SIDE), shift(a, 1, SIDE)
    bm, bp, bo = shift(b, -1, SIDE), shift(b, 1, SIDE), shift(b, 2, SIDE)

    first_copies = [
        pltpu.make_async_copy(k_hbm, kv.at[core, 0, b, a, 0, pl.ds(0, SHARD)], in_sem.at[0]),
        pltpu.make_async_copy(v_hbm, kv.at[core, 0, b, a, 1, pl.ds(0, SHARD)], in_sem.at[1]),
    ]
    q_copies = [
        pltpu.make_async_copy(source, q_in.at[n], in_sem.at[2 + n])
        for n, source in enumerate((q1_hbm, q2_hbm))
    ]
    for copy in first_copies + q_copies:
        copy.start()

    barrier = pltpu.get_barrier_semaphore()
    for device in (*along_z.values(), dev_ap, dev_am, dev_bp, dev_bm, dev_sib):
        pl.semaphore_signal(barrier, inc=1, device_id=device, device_id_type=MESH)
    for copy in first_copies:
        copy.wait()
    pl.semaphore_wait(barrier, 9)

    def remote(src, dst, send, recv, device):
        return pltpu.make_async_remote_copy(
            src_ref=src,
            dst_ref=dst,
            send_sem=send,
            recv_sem=recv,
            device_id=device,
            device_id_type=MESH,
        )

    def shard(g, half):
        return kv.at[core, g, b, a, :, pl.ds(half * SHARD, SHARD)]

    def z_move(source, by, target):
        g, half = place_of(target)
        return remote(
            shard(*place_of(source)), shard(g, half), z_send.at[g, half], z_recv.at[g, half], along_z[by]
        )

    starts = [z_move(0, -by, by) for by in (1, -1, 2, -2)]
    onward = {source: z_move(source, by, target) for source, by, target in ONWARD}
    arrivals = {target: move for move, target in zip(starts, (1, -1, 2, -2))}
    arrivals.update({target: onward[source] for source, _, target in ONWARD})

    def own(g, way):
        piece = kv.at[core, g, b, a]
        return remote(piece, piece, a_send.at[way, g], a_recv.at[way, g], (dev_ap, dev_am)[way])

    def a_on(g, way):
        piece = kv.at[core, g, b, (am, ap)[way], way]
        return remote(piece, piece, a_send.at[2 + way, g], a_recv.at[2 + way, g], (dev_ap, dev_am)[way])

    def row_out(g, way):
        piece = kv.at[core, g, b]
        return remote(piece, piece, b_send.at[way, g], b_recv.at[way, g], (dev_bp, dev_bm)[way])

    def b_on(g, way):
        piece = kv.at[core, g, (bm, bp)[way], :, way]
        return remote(piece, piece, b_send.at[2 + way, g], b_recv.at[2 + way, g], (dev_bp, dev_bm)[way])

    def across(g, which):
        piece = kv.at[core, g, (b, bm, bp, bo)[which]]
        return remote(piece, piece, s_send.at[which, g], s_recv.at[which, g], dev_sib)

    def hop(n):
        which, group, half = HOPS[n]
        member = RELATIVE[group][half]
        source_group, source_half = place_of(member - 1 if which == 0 else member + 1)
        source = kv.at[core, source_group, :, :, which, pl.ds(source_half * SHARD, SHARD)]
        target = kv.at[core, group, :, :, which, pl.ds(half * SHARD, SHARD)]
        device = along_z[-1 if which == 0 else 1]
        return source_group, remote(source, target, hop_send.at[n], hop_recv.at[n], device)

    def across_hopped(g):
        piece = kv.at[core, g]
        n = g - GROUPS
        return remote(piece, piece, s_send.at[4, n], s_recv.at[4, n], dev_sib)

    for move in starts:
        move.start()

    def stage_own(g):
        for group, members in enumerate(ROUND):

            @pl.when(g == group)
            def _(group=group, members=members):
                waited = (1, -1) if group == 0 else tuple(m for m in members if m != -1)
                for member in waited:
                    arrivals[member].wait_recv()
                    if member in onward:
                        onward[member].start()

        own(g, 0).start()
        own(g, 1).start()

    def stage_a1(g):
        for way in (0, 1):
            own(g, way).wait_recv()
            a_on(g, way).start()

    def stage_a2(g):
        for way in (0, 1):
            a_on(g, way).wait_recv()
        for way in (0, 1):
            row_out(g, way).start()
        across(g, 0).start()

    def stage_b1(g):
        for way in (0, 1):
            row_out(g, way).wait_recv()
            b_on(g, way).start()
            across(g, 1 + way).start()

    def stage_b2(g):
        for way in (0, 1):
            b_on(g, way).wait_recv()
        across(g, 3).start()
        for n in range(len(HOPS)):
            source_group, copy = hop(n)

            @pl.when(g == source_group)
            def _(copy=copy):
                copy.start()

    def stage_hopped(g):
        for n, (_, group, _) in enumerate(HOPS):

            @pl.when(g == group)
            def _(n=n):
                hop(n)[1].wait_recv()

        across_hopped(g).start()

    def select(g, half):
        value = jnp.int32(0)
        for group, members in enumerate(RELATIVE):
            value = jnp.where(g == group, members[half], value)
        return value

    def prepare(step):
        if step < 2:
            q_copies[step].wait()
            q_rows[step * LAYER_ROWS : (step + 1) * LAYER_ROWS] = q_in[step].reshape(LAYER_ROWS, WIDTH)
        elif step == 2:
            row_max[...] = jnp.full_like(row_max, FLOOR)
            row_sum[...] = jnp.zeros_like(row_sum)
        else:
            acc[...] = jnp.zeros_like(acc)

    def attend(g, layer, last):
        def keys_of(which):
            pieces = []
            for x_key in range(last + 1):
                pieces.append(kv[0, g, :, x_key, which].reshape(HALF, WIDTH))
                pieces.append(kv[1, g, x_key, :, which].reshape(HALF, WIDTH))
            return jnp.concatenate(pieces, axis=0)

        keys = keys_of(0)
        values = keys_of(1)
        at = lax.broadcasted_iota(jnp.int32, (1, 2 * HALF), 1)
        from_core = at // HALF
        y_key = lax.rem(at // GROUP_ROWS, SIDE)
        z_rel = jnp.where(lax.rem(at // SHARD, 2) == 0, select(g, 0), select(g, 1))
        z_key = lax.rem(z + z_rel + DEPTH, DEPTH)
        key_pos = ((last * SIDE + y_key) * 2 + from_core) * BLOCK + z_key * SHARD + lax.rem(at, SHARD)
        open_width = 2 * HALF * last
        lanes = 2 * (last + 1)
        start = layer * LAYER_ROWS
        for tile in range(LAYER_ROWS // TILE):
            here = pl.ds(pl.multiple_of(start + tile * TILE, TILE), TILE)
            scores = lax.dot_general(
                q_rows[here], keys, (((1,), (1,)), ((), ())), preferred_element_type=jnp.float32
            )
            row = lax.broadcasted_iota(jnp.int32, (TILE, 1), 0) + tile * TILE
            allowed = key_pos <= place * BLOCK + row // 2
            edge = jnp.where(allowed, scores[:, open_width:], MASKED)
            pieces = [scores[:, n * 128 : (n + 1) * 128] for n in range(lanes - 2)]
            pieces += [edge[:, :128], edge[:, 128:]]
            peak = functools.reduce(jnp.maximum, pieces)
            old = row_max[here]
            new = jnp.maximum(old, jnp.max(peak, axis=1, keepdims=True))
            fade = jnp.exp2((old - new) * scale2)
            weights = [jnp.exp2((piece - new) * scale2) for piece in pieces]
            row_max[here] = new
            row_sum[here] = row_sum[here] * fade + functools.reduce(jnp.add, weights)
            rounded = jnp.concatenate([w.astype(jnp.bfloat16) for w in weights], axis=1)
            mixed = jnp.dot(rounded, values, preferred_element_type=jnp.float32)
            acc[here] = acc[here] * jnp.concatenate((fade, fade), axis=1) + mixed

    def use(g, layer):
        for last in range(SIDE):

            @pl.when(x == last)
            def _(last=last):
                attend(g, layer, last)

    def stage_use(g):
        for which in range(4):
            across(g, which).wait_recv()
        use(g, 0)

    def drain(g):
        for way in (0, 1):
            own(g, way).wait_send()
            a_on(g, way).wait_send()
            row_out(g, way).wait_send()
            b_on(g, way).wait_send()
        for which in range(4):
            across(g, which).wait_send()

    stages = (
        (OFF_OWN, stage_own),
        (OFF_A1, stage_a1),
        (OFF_A2, stage_a2),
        (OFF_USE, stage_use),
        (OFF_B1, stage_b1),
        (OFF_B2, stage_b2),
    )
    hop_tick = TICKS - len(HOPPED)

    @pl.loop(0, TICKS)
    def _(tick):
        for offset, stage in stages:
            g = tick - offset

            @pl.when((g >= 0) & (g < GROUPS))
            def _(stage=stage, g=g):
                stage(g)

        for step in range(4):

            @pl.when(tick == step)
            def _(step=step):
                prepare(step)

        hopped = tick >= hop_tick
        hop_group = jnp.where(hopped, tick - hop_tick + GROUPS, GROUPS)

        @pl.when(hopped)
        def _():
            stage_hopped(hop_group)

        @pl.loop(0, jnp.where(hopped, 3, jnp.where(tick >= OFF_USE, 1, 0)))
        def _(item):
            @pl.when(item == 1)
            def _():
                across_hopped(hop_group).wait_recv()
                use(hop_group, 0)

            @pl.when(item != 1)
            def _():
                use(jnp.where(item == 0, tick - OFF_USE, hop_group), 1)

    for move in arrivals.values():
        move.wait_send()
    for n in range(len(HOPS)):
        hop(n)[1].wait_send()
    for g in range(GROUPS, len(RELATIVE)):
        across_hopped(g).wait_send()

    @pl.loop(0, GROUPS)
    def _(g):
        drain(g)

    for layer, o_ref in enumerate((o1_ref, o2_ref)):
        for part in range(LAYER_ROWS // TILE):
            here = pl.ds(layer * LAYER_ROWS + part * TILE, TILE)
            inverse = 1.0 / jnp.sum(row_sum[here], axis=1, keepdims=True)
            o_ref[part * TILE : (part + 1) * TILE] = (acc[here] * inverse).astype(jnp.bfloat16)


def on_device(queries_first, queries_second, shared_keys, shared_values):
    tokens_here, heads, width = queries_first.shape
    rows = 2 * tokens_here * heads
    scale2 = math.log2(math.e) / math.sqrt(width)
    dma = pltpu.SemaphoreType.DMA
    out = jax.ShapeDtypeStruct((rows // 2, width), jnp.bfloat16)
    vmem = pl.BlockSpec(memory_space=pltpu.VMEM)
    result = pl.pallas_call(
        functools.partial(attention_kernel, scale2),
        out_shape=(out, out),
        in_specs=[pl.BlockSpec(memory_space=pl.ANY)] * 4,
        out_specs=(vmem, vmem),
        scratch_shapes=[
            pltpu.VMEM((2, len(RELATIVE), SIDE, SIDE, 2, GROUP_ROWS, width), jnp.bfloat16),
            pltpu.VMEM((2, tokens_here, heads, width), jnp.bfloat16),
            pltpu.VMEM((rows, width), jnp.bfloat16),
            pltpu.VMEM((rows, 128), jnp.float32),
            pltpu.VMEM((rows, 128), jnp.float32),
            pltpu.VMEM((rows, width), jnp.float32),
            dma((4,)),
            dma((GROUPS, 2)),
            dma((GROUPS, 2)),
            dma((4, GROUPS)),
            dma((4, GROUPS)),
            dma((4, GROUPS)),
            dma((4, GROUPS)),
            dma((5, GROUPS)),
            dma((5, GROUPS)),
            dma((len(HOPS),)),
            dma((len(HOPS),)),
        ],
        compiler_params=pltpu.CompilerParams(
            collective_id=0, has_side_effects=True, vmem_limit_bytes=56 * 1024 * 1024
        ),
        cost_estimate=pl.CostEstimate(
            flops=4 * rows * 8192 * width, bytes_accessed=1 << 20, transcendentals=rows * 8192
        ),
    )(queries_first, queries_second, shared_keys, shared_values)
    return tuple(array.reshape(tokens_here, heads, width) for array in result)


def solution(mesh):
    return jax.shard_map(
        on_device,
        mesh=mesh,
        in_specs=(
            P("inner", "outer", None),
            P("inner", "outer", None),
            P(("inner", "outer"), None),
            P(("inner", "outer"), None),
        ),
        out_specs=(P("inner", "outer", None), P("inner", "outer", None)),
        check_vma=False,
    )
```

```python
import functools
import math

import jax
import jax.numpy as jnp
from jax import lax
from jax.experimental import pallas as pl
from jax.experimental.pallas import tpu as pltpu
from jax.sharding import PartitionSpec as P

MESH = pl.DeviceIdType.MESH
MASKED = -1e30
FLOOR = -1e20
SIDE = 4
DEPTH = 16
SHARD = 16
GROUP_ROWS = 2 * SHARD
BLOCK = DEPTH * SHARD
HALF = SIDE * GROUP_ROWS
LAYER_ROWS = 2 * BLOCK
ROWS = 2 * LAYER_ROWS
WIDTH = 256
ROUND = ((0, 1), (3, -3), (5, -5), (7, -7), (-1, 2), (-2, 8))
HOPPED = ((4, -4), (6, -6))
RELATIVE = ROUND + HOPPED
GROUPS = len(ROUND)
HOPS = tuple(
    (which, group, half)
    for group in range(GROUPS, len(RELATIVE))
    for which in (0, 1)
    for half in (0, 1)
)
ONWARD = ((1, -2, 3), (-1, 2, -3), (3, -2, 5), (-3, 2, -5), (5, -2, 7), (-5, 2, -7), (7, -1, 8))
OFF_OWN, OFF_A1, OFF_A2, OFF_B1, OFF_B2 = 0, 1, 2, 3, 4
TICKS = GROUPS + OFF_B2
MINE, SIBLING = 0, 1
ITEMS = (
    (4, 0, SIBLING),
    (5, 1, SIBLING),
    (5, 0, MINE),
    (6, 2, SIBLING),
    (6, 1, MINE),
    (7, 3, SIBLING),
    (7, 2, MINE),
    (8, 4, SIBLING),
    (8, 3, MINE),
    (8, 6, SIBLING),
    (8, 6, MINE),
    (9, 5, SIBLING),
    (9, 7, SIBLING),
    (9, 4, MINE),
    (9, 5, MINE),
    (9, 7, MINE),
)
HAND_OVER = 13
TILE = 256


def place_of(relative):
    for group, members in enumerate(RELATIVE):
        for half, member in enumerate(members):
            if member % DEPTH == relative % DEPTH:
                return group, half
    return None


def attention_kernel(
    scale2,
    q1_hbm,
    q2_hbm,
    k_hbm,
    v_hbm,
    o1_ref,
    o2_ref,
    kv,
    q_in,
    q_rows,
    row_max,
    row_sum,
    acc,
    acc_out,
    acc_in,
    stat_out,
    stat_in,
    in_sem,
    z_send,
    z_recv,
    a_send,
    a_recv,
    b_send,
    b_recv,
    pair_send,
    pair_recv,
    hop_send,
    hop_recv,
):
    z = lax.axis_index("outer")
    place = lax.axis_index("inner")
    core = lax.rem(place, 2)
    chip = place // 2
    x = chip // SIDE
    y = lax.rem(chip, SIDE)
    flip = 1 - core
    a = x * flip + y * core
    b = y * flip + x * core

    def shift(value, by, size):
        return lax.rem(value + by + size, size)

    def inner_of(a_place, b_place):
        x_place = a_place * flip + b_place * core
        y_place = b_place * flip + a_place * core
        return (x_place * SIDE + y_place) * 2 + core

    along_z = {by: (shift(z, by, DEPTH), place) for by in (-2, -1, 1, 2)}
    dev_ap = (z, inner_of(shift(a, 1, SIDE), b))
    dev_am = (z, inner_of(shift(a, -1, SIDE), b))
    dev_bp = (z, inner_of(a, shift(b, 1, SIDE)))
    dev_bm = (z, inner_of(a, shift(b, -1, SIDE)))
    dev_sib = (z, place + 1 - 2 * core)
    am, ap = shift(a, -1, SIDE), shift(a, 1, SIDE)
    bm, bp, bo = shift(b, -1, SIDE), shift(b, 1, SIDE), shift(b, 2, SIDE)

    first_copies = [
        pltpu.make_async_copy(k_hbm, kv.at[core, 0, b, a, 0, pl.ds(0, SHARD)], in_sem.at[0]),
        pltpu.make_async_copy(v_hbm, kv.at[core, 0, b, a, 1, pl.ds(0, SHARD)], in_sem.at[1]),
    ]
    q_copies = [
        pltpu.make_async_copy(source, q_in.at[n], in_sem.at[2 + n])
        for n, source in enumerate((q1_hbm, q2_hbm))
    ]
    for copy in first_copies + q_copies:
        copy.start()

    barrier = pltpu.get_barrier_semaphore()
    for device in (*along_z.values(), dev_ap, dev_am, dev_bp, dev_bm, dev_sib):
        pl.semaphore_signal(barrier, inc=1, device_id=device, device_id_type=MESH)
    for copy in first_copies:
        copy.wait()
    pl.semaphore_wait(barrier, 9)

    def remote(src, dst, send, recv, device):
        return pltpu.make_async_remote_copy(
            src_ref=src,
            dst_ref=dst,
            send_sem=send,
            recv_sem=recv,
            device_id=device,
            device_id_type=MESH,
        )

    def shard(g, half):
        return kv.at[core, g, b, a, :, pl.ds(half * SHARD, SHARD)]

    def z_move(source, by, target):
        g, half = place_of(target)
        return remote(
            shard(*place_of(source)), shard(g, half), z_send.at[g, half], z_recv.at[g, half], along_z[by]
        )

    starts = [z_move(0, -by, by) for by in (1, -1, 2, -2)]
    onward = {source: z_move(source, by, target) for source, by, target in ONWARD}
    arrivals = {target: move for move, target in zip(starts, (1, -1, 2, -2))}
    arrivals.update({target: onward[source] for source, _, target in ONWARD})

    def own(g, way):
        piece = kv.at[core, g, b, a]
        return remote(piece, piece, a_send.at[way, g], a_recv.at[way, g], (dev_ap, dev_am)[way])

    def a_on(g, way):
        piece = kv.at[core, g, b, (am, ap)[way], way]
        return remote(piece, piece, a_send.at[2 + way, g], a_recv.at[2 + way, g], (dev_ap, dev_am)[way])

    def row_out(g, way):
        piece = kv.at[core, g, b]
        return remote(piece, piece, b_send.at[way, g], b_recv.at[way, g], (dev_bp, dev_bm)[way])

    def b_on(g, way):
        piece = kv.at[core, g, (bm, bp)[way], :, way]
        return remote(piece, piece, b_send.at[2 + way, g], b_recv.at[2 + way, g], (dev_bp, dev_bm)[way])

    mine, theirs = pl.ds(0, ROWS), pl.ds(ROWS, ROWS)
    q_across = remote(q_rows.at[mine], q_rows.at[theirs], pair_send.at[0], pair_recv.at[0], dev_sib)
    acc_across = remote(acc_out, acc_in, pair_send.at[1], pair_recv.at[1], dev_sib)
    stat_across = remote(stat_out, stat_in, pair_send.at[2], pair_recv.at[2], dev_sib)

    def hop(n):
        which, group, half = HOPS[n]
        member = RELATIVE[group][half]
        source_group, source_half = place_of(member - 1 if which == 0 else member + 1)
        source = kv.at[core, source_group, :, :, which, pl.ds(source_half * SHARD, SHARD)]
        target = kv.at[core, group, :, :, which, pl.ds(half * SHARD, SHARD)]
        device = along_z[-1 if which == 0 else 1]
        return source_group, remote(source, target, hop_send.at[n], hop_recv.at[n], device)

    for move in starts:
        move.start()

    def stage_own(g):
        for group, members in enumerate(ROUND):

            @pl.when(g == group)
            def _(group=group, members=members):
                waited = (1, -1) if group == 0 else tuple(m for m in members if m != -1)
                for member in waited:
                    arrivals[member].wait_recv()
                    if member in onward:
                        onward[member].start()

        own(g, 0).start()
        own(g, 1).start()

    def stage_a1(g):
        for way in (0, 1):
            own(g, way).wait_recv()
            a_on(g, way).start()

    def stage_a2(g):
        for way in (0, 1):
            a_on(g, way).wait_recv()
        for way in (0, 1):
            row_out(g, way).start()

    def stage_b1(g):
        for way in (0, 1):
            row_out(g, way).wait_recv()
            b_on(g, way).start()

    def stage_b2(g):
        for way in (0, 1):
            b_on(g, way).wait_recv()
        for n in range(len(HOPS)):
            source_group, copy = hop(n)

            @pl.when(g == source_group)
            def _(copy=copy):
                copy.start()

    def select(g, half):
        value = jnp.int32(0)
        for group, members in enumerate(RELATIVE):
            value = jnp.where(g == group, members[half], value)
        return value

    def prepare(step):
        if step < 2:
            q_copies[step].wait()
            q_rows[step * LAYER_ROWS : (step + 1) * LAYER_ROWS] = q_in[step].reshape(LAYER_ROWS, WIDTH)
            if step == 1:
                q_across.start()
        else:
            part = pl.ds((step - 2) * ROWS, ROWS)
            acc[part] = jnp.zeros((ROWS, WIDTH), jnp.float32)
            row_max[part] = jnp.full((ROWS, 128), FLOOR, jnp.float32)
            row_sum[part] = jnp.zeros((ROWS, 128), jnp.float32)

    def attend(g, layer, token_block, last):
        def keys_of(which):
            pieces = []
            for x_key in range(last + 1):
                for y_key in range(SIDE):
                    row = y_key * flip + x_key * core
                    column = x_key * flip + y_key * core
                    pieces.append(kv[core, g, row, column, which])
            return jnp.concatenate(pieces, axis=0)

        keys = keys_of(0)
        values = keys_of(1)
        at = lax.broadcasted_iota(jnp.int32, (1, HALF), 1)
        y_key = at // GROUP_ROWS
        z_rel = jnp.where(lax.rem(at // SHARD, 2) == 0, select(g, 0), select(g, 1))
        z_key = lax.rem(z + z_rel + DEPTH, DEPTH)
        key_pos = ((last * SIDE + y_key) * 2 + core) * BLOCK + z_key * SHARD + lax.rem(at, SHARD)
        open_width = HALF * last
        start = layer * LAYER_ROWS
        for tile in range(LAYER_ROWS // TILE):
            here = pl.ds(start + tile * TILE, TILE)
            scores = lax.dot_general(
                q_rows[here], keys, (((1,), (1,)), ((), ())), preferred_element_type=jnp.float32
            )
            row = lax.broadcasted_iota(jnp.int32, (TILE, 1), 0) + tile * TILE
            allowed = key_pos <= token_block * BLOCK + row // 2
            edge = jnp.where(allowed, scores[:, open_width:], MASKED)
            pieces = [scores[:, n * HALF : (n + 1) * HALF] for n in range(last)] + [edge]
            peak = functools.reduce(jnp.maximum, pieces)
            old = row_max[here]
            new = jnp.maximum(old, jnp.max(peak, axis=1, keepdims=True))
            fade = jnp.exp2((old - new) * scale2)
            weights = [jnp.exp2((piece - new) * scale2) for piece in pieces]
            row_max[here] = new
            row_sum[here] = row_sum[here] * fade + functools.reduce(jnp.add, weights)
            rounded = jnp.concatenate([w.astype(jnp.bfloat16) for w in weights], axis=1)
            mixed = jnp.dot(rounded, values, preferred_element_type=jnp.float32)
            acc[here] = acc[here] * jnp.concatenate((fade, fade), axis=1) + mixed

    def use(g, rows):
        token_block = place if rows == MINE else place + 1 - 2 * core
        for last in range(SIDE):

            @pl.when(x == last)
            def _(last=last):
                for layer in (2 * rows, 2 * rows + 1):
                    attend(g, layer, token_block, last)

    row_at = lax.broadcasted_iota(jnp.int32, (128, 128), 0)
    diagonal = row_at == lax.broadcasted_iota(jnp.int32, (128, 128), 1)

    def hand_over():
        acc_out[...] = acc[theirs].astype(jnp.bfloat16)
        acc_across.start()
        count = ROWS // 128
        for block in range(count):
            there = pl.ds(ROWS + block * 128, 128)
            total = jnp.sum(row_sum[there], axis=1, keepdims=True)
            for n, value in ((block, row_max[there]), (count + block, total)):
                stat_out[n : n + 1] = jnp.sum(
                    jnp.where(diagonal, value, 0.0), axis=0, keepdims=True
                )
        stat_across.start()

    def drain(g):
        for way in (0, 1):
            own(g, way).wait_send()
            a_on(g, way).wait_send()
            row_out(g, way).wait_send()
            b_on(g, way).wait_send()

    stages = (
        (OFF_OWN, stage_own),
        (OFF_A1, stage_a1),
        (OFF_A2, stage_a2),
        (OFF_B1, stage_b1),
        (OFF_B2, stage_b2),
    )

    def pick(index, table):
        value = jnp.int32(0)
        for n, entry in enumerate(table):
            value = jnp.where(index == n, entry, value)
        return value

    begins = [sum(tick < at for tick, _, _ in ITEMS) for at in range(TICKS + 1)]

    @pl.loop(0, TICKS)
    def _(tick):
        for offset, stage in stages:
            g = tick - offset

            @pl.when((g >= 0) & (g < GROUPS))
            def _(stage=stage, g=g):
                stage(g)

        for step in range(4):

            @pl.when(tick == step)
            def _(step=step):
                prepare(step)

        @pl.loop(pick(tick, begins), pick(tick + 1, begins))
        def _(item):
            @pl.when(item == 0)
            def _():
                q_across.wait_recv()

            for n, (_, group, _) in enumerate(HOPS):

                @pl.when(item == ITEMS.index((8 if group == GROUPS else 9, group, SIBLING)))
                def _(n=n):
                    hop(n)[1].wait_recv()

            @pl.when(item == HAND_OVER)
            def _():
                hand_over()

            group = pick(item, [group for _, group, _ in ITEMS])
            rows = pick(item, [rows for _, _, rows in ITEMS])
            for choice in (MINE, SIBLING):

                @pl.when(rows == choice)
                def _(choice=choice):
                    use(group, choice)

    for move in arrivals.values():
        move.wait_send()
    for n in range(len(HOPS)):
        hop(n)[1].wait_send()
    q_across.wait_send()

    @pl.loop(0, GROUPS)
    def _(g):
        drain(g)

    stat_across.wait()
    acc_across.wait()
    count = ROWS // 128
    for layer, o_ref in enumerate((o1_ref, o2_ref)):
        for part in range(LAYER_ROWS // 128):
            block = layer * (LAYER_ROWS // 128) + part
            here = pl.ds(block * 128, 128)

            def column(n):
                return jnp.sum(jnp.where(diagonal, stat_in[n : n + 1], 0.0), axis=1, keepdims=True)

            own_max, other_max = row_max[here][:, :1], column(block)
            peak = jnp.maximum(own_max, other_max)
            keep = jnp.exp2((own_max - peak) * scale2)
            add = jnp.exp2((other_max - peak) * scale2)
            total = jnp.sum(row_sum[here], axis=1, keepdims=True) * keep + column(count + block) * add
            inverse = 1.0 / total
            result = acc[here] * (keep * inverse) + acc_in[here].astype(jnp.float32) * (add * inverse)
            o_ref[part * 128 : (part + 1) * 128] = result.astype(jnp.bfloat16)


def on_device(queries_first, queries_second, shared_keys, shared_values):
    tokens_here, heads, width = queries_first.shape
    rows = 2 * tokens_here * heads
    scale2 = math.log2(math.e) / math.sqrt(width)
    dma = pltpu.SemaphoreType.DMA
    out = jax.ShapeDtypeStruct((rows // 2, width), jnp.bfloat16)
    vmem = pl.BlockSpec(memory_space=pltpu.VMEM)
    result = pl.pallas_call(
        functools.partial(attention_kernel, scale2),
        out_shape=(out, out),
        in_specs=[pl.BlockSpec(memory_space=pl.ANY)] * 4,
        out_specs=(vmem, vmem),
        scratch_shapes=[
            pltpu.VMEM((2, len(RELATIVE), SIDE, SIDE, 2, GROUP_ROWS, width), jnp.bfloat16),
            pltpu.VMEM((2, tokens_here, heads, width), jnp.bfloat16),
            pltpu.VMEM((2 * rows, width), jnp.bfloat16),
            pltpu.VMEM((2 * rows, 128), jnp.float32),
            pltpu.VMEM((2 * rows, 128), jnp.float32),
            pltpu.VMEM((2 * rows, width), jnp.float32),
            pltpu.VMEM((rows, width), jnp.bfloat16),
            pltpu.VMEM((rows, width), jnp.bfloat16),
            pltpu.VMEM((2 * rows // 128, 128), jnp.float32),
            pltpu.VMEM((2 * rows // 128, 128), jnp.float32),
            dma((4,)),
            dma((GROUPS, 2)),
            dma((GROUPS, 2)),
            dma((4, GROUPS)),
            dma((4, GROUPS)),
            dma((4, GROUPS)),
            dma((4, GROUPS)),
            dma((3,)),
            dma((3,)),
            dma((len(HOPS),)),
            dma((len(HOPS),)),
        ],
        compiler_params=pltpu.CompilerParams(
            collective_id=0, has_side_effects=True, vmem_limit_bytes=56 * 1024 * 1024
        ),
        cost_estimate=pl.CostEstimate(
            flops=4 * rows * 8192 * width, bytes_accessed=1 << 20, transcendentals=rows * 8192
        ),
    )(queries_first, queries_second, shared_keys, shared_values)
    return tuple(array.reshape(tokens_here, heads, width) for array in result)


def solution(mesh):
    return jax.shard_map(
        on_device,
        mesh=mesh,
        in_specs=(
            P("inner", "outer", None),
            P("inner", "outer", None),
            P(("inner", "outer"), None),
            P(("inner", "outer"), None),
        ),
        out_specs=(P("inner", "outer", None), P("inner", "outer", None)),
        check_vma=False,
    )
```

```python
import functools
import math

import jax
import jax.numpy as jnp
from jax import lax
from jax.experimental import pallas as pl
from jax.experimental.pallas import tpu as pltpu
from jax.sharding import PartitionSpec as P

MESH = pl.DeviceIdType.MESH
MASKED = -1e30
FLOOR = -1e20
SIDE = 4
DEPTH = 16
SHARD = 16
GROUP_ROWS = 2 * SHARD
BLOCK = DEPTH * SHARD
HALF = SIDE * GROUP_ROWS
LAYER_ROWS = 2 * BLOCK
ROWS = 2 * LAYER_ROWS
WIDTH = 256
ROUND = ((0, 1), (3, -3), (5, -5), (7, -7), (-1, 2), (-2, 8))
HOPPED = ((4, -4), (6, -6))
RELATIVE = ROUND + HOPPED
GROUPS = len(ROUND)
HOPS = tuple(
    (which, group, half)
    for group in range(GROUPS, len(RELATIVE))
    for which in (0, 1)
    for half in (0, 1)
)
ONWARD = ((1, -2, 3), (-1, 2, -3), (3, -2, 5), (-3, 2, -5), (5, -2, 7), (-5, 2, -7), (7, -1, 8))
OFF_OWN, OFF_A1, OFF_A2, OFF_B1, OFF_B2 = 0, 1, 2, 4, 5
TICKS = GROUPS + OFF_B2 + 1
MINE, SIBLING = 0, 1
ITEMS = (
    (6, 0, SIBLING),
    (7, 1, SIBLING),
    (7, 0, MINE),
    (8, 2, SIBLING),
    (8, 1, MINE),
    (9, 3, SIBLING),
    (9, 2, MINE),
    (10, 4, SIBLING),
    (10, 3, MINE),
    (10, 6, SIBLING),
    (10, 4, MINE),
    (10, 6, MINE),
    (10, 7, SIBLING),
    (11, 5, SIBLING),
    (11, 7, MINE),
    (11, 5, MINE),
)
HAND_OVER = 14
TILE = 256


def place_of(relative):
    for group, members in enumerate(RELATIVE):
        for half, member in enumerate(members):
            if member % DEPTH == relative % DEPTH:
                return group, half
    return None


def attention_kernel(
    scale2,
    q1_hbm,
    q2_hbm,
    k_hbm,
    v_hbm,
    o1_ref,
    o2_ref,
    kv,
    q_in,
    q_rows,
    row_max,
    row_sum,
    acc,
    acc_out,
    acc_in,
    stat_out,
    stat_in,
    in_sem,
    z_send,
    z_recv,
    a_send,
    a_recv,
    b_send,
    b_recv,
    pair_send,
    pair_recv,
    hop_send,
    hop_recv,
):
    z = lax.axis_index("outer")
    place = lax.axis_index("inner")
    core = lax.rem(place, 2)
    chip = place // 2
    x = chip // SIDE
    y = lax.rem(chip, SIDE)
    flip = 1 - core
    a = x * flip + y * core
    b = y * flip + x * core

    def shift(value, by, size):
        return lax.rem(value + by + size, size)

    def inner_of(a_place, b_place):
        x_place = a_place * flip + b_place * core
        y_place = b_place * flip + a_place * core
        return (x_place * SIDE + y_place) * 2 + core

    along_z = {by: (shift(z, by, DEPTH), place) for by in (-2, -1, 1, 2)}
    dev_ap = (z, inner_of(shift(a, 1, SIDE), b))
    dev_am = (z, inner_of(shift(a, -1, SIDE), b))
    dev_bp = (z, inner_of(a, shift(b, 1, SIDE)))
    dev_bm = (z, inner_of(a, shift(b, -1, SIDE)))
    dev_sib = (z, place + 1 - 2 * core)
    am, ap = shift(a, -1, SIDE), shift(a, 1, SIDE)
    bm, bp, bo = shift(b, -1, SIDE), shift(b, 1, SIDE), shift(b, 2, SIDE)

    first_copies = [
        pltpu.make_async_copy(k_hbm, kv.at[core, 0, b, a, 0, pl.ds(0, SHARD)], in_sem.at[0]),
        pltpu.make_async_copy(v_hbm, kv.at[core, 0, b, a, 1, pl.ds(0, SHARD)], in_sem.at[1]),
    ]
    q_copies = [
        pltpu.make_async_copy(source, q_in.at[n], in_sem.at[2 + n])
        for n, source in enumerate((q1_hbm, q2_hbm))
    ]
    for copy in first_copies + q_copies:
        copy.start()

    barrier = pltpu.get_barrier_semaphore()
    for device in (*along_z.values(), dev_ap, dev_am, dev_bp, dev_bm, dev_sib):
        pl.semaphore_signal(barrier, inc=1, device_id=device, device_id_type=MESH)
    for copy in first_copies:
        copy.wait()
    pl.semaphore_wait(barrier, 9)

    def remote(src, dst, send, recv, device):
        return pltpu.make_async_remote_copy(
            src_ref=src,
            dst_ref=dst,
            send_sem=send,
            recv_sem=recv,
            device_id=device,
            device_id_type=MESH,
        )

    def shard(g, half):
        return kv.at[core, g, b, a, :, pl.ds(half * SHARD, SHARD)]

    def z_move(source, by, target):
        g, half = place_of(target)
        return remote(
            shard(*place_of(source)), shard(g, half), z_send.at[g, half], z_recv.at[g, half], along_z[by]
        )

    starts = [z_move(0, -by, by) for by in (1, -1, 2, -2)]
    onward = {source: z_move(source, by, target) for source, by, target in ONWARD}
    arrivals = {target: move for move, target in zip(starts, (1, -1, 2, -2))}
    arrivals.update({target: onward[source] for source, _, target in ONWARD})

    def own(g, way):
        piece = kv.at[core, g, b, a]
        return remote(piece, piece, a_send.at[way, g], a_recv.at[way, g], (dev_ap, dev_am)[way])

    def a_on(g, way):
        piece = kv.at[core, g, b, (am, ap)[way], way]
        return remote(piece, piece, a_send.at[2 + way, g], a_recv.at[2 + way, g], (dev_ap, dev_am)[way])

    def row_out(g, way):
        piece = kv.at[core, g, b]
        return remote(piece, piece, b_send.at[way, g], b_recv.at[way, g], (dev_bp, dev_bm)[way])

    def b_on(g, way):
        piece = kv.at[core, g, (bm, bp)[way], :, way]
        return remote(piece, piece, b_send.at[2 + way, g], b_recv.at[2 + way, g], (dev_bp, dev_bm)[way])

    mine, theirs = pl.ds(0, ROWS), pl.ds(ROWS, ROWS)
    q_across = remote(q_rows.at[mine], q_rows.at[theirs], pair_send.at[0], pair_recv.at[0], dev_sib)
    acc_across = remote(acc_out, acc_in, pair_send.at[1], pair_recv.at[1], dev_sib)
    stat_across = remote(stat_out, stat_in, pair_send.at[2], pair_recv.at[2], dev_sib)

    def hop(n):
        which, group, half = HOPS[n]
        member = RELATIVE[group][half]
        source_group, source_half = place_of(member - 1 if which == 0 else member + 1)
        source = kv.at[core, source_group, :, :, which, pl.ds(source_half * SHARD, SHARD)]
        target = kv.at[core, group, :, :, which, pl.ds(half * SHARD, SHARD)]
        device = along_z[-1 if which == 0 else 1]
        return source_group, remote(source, target, hop_send.at[n], hop_recv.at[n], device)

    for move in starts:
        move.start()

    def stage_own(g):
        for group, members in enumerate(ROUND):

            @pl.when(g == group)
            def _(group=group, members=members):
                waited = (1, -1) if group == 0 else tuple(m for m in members if m != -1)
                for member in waited:
                    arrivals[member].wait_recv()
                    if member in onward:
                        onward[member].start()

        own(g, 0).start()
        own(g, 1).start()

    def stage_a1(g):
        for way in (0, 1):
            own(g, way).wait_recv()
            a_on(g, way).start()

    def stage_a2(g):
        for way in (0, 1):
            a_on(g, way).wait_recv()
        for way in (0, 1):
            row_out(g, way).start()

    def stage_b1(g):
        for way in (0, 1):
            row_out(g, way).wait_recv()
            b_on(g, way).start()

    def stage_b2(g):
        for way in (0, 1):
            b_on(g, way).wait_recv()
        for n in range(len(HOPS)):
            source_group, copy = hop(n)

            @pl.when(g == source_group)
            def _(copy=copy):
                copy.start()

    def select(g, half):
        value = jnp.int32(0)
        for group, members in enumerate(RELATIVE):
            value = jnp.where(g == group, members[half], value)
        return value

    def prepare(step):
        if step < 2:
            q_copies[step].wait()
            q_rows[step * LAYER_ROWS : (step + 1) * LAYER_ROWS] = q_in[step].reshape(LAYER_ROWS, WIDTH)
            if step == 1:
                q_across.start()
        else:
            part = pl.ds((step - 2) * ROWS, ROWS)
            acc[part] = jnp.zeros((ROWS, WIDTH), jnp.float32)
            row_max[part] = jnp.full((ROWS, 128), FLOOR, jnp.float32)
            row_sum[part] = jnp.zeros((ROWS, 128), jnp.float32)

    def attend(g, layer, token_block, last):
        def keys_of(which):
            pieces = []
            for x_key in range(last + 1):
                for y_key in range(SIDE):
                    row = y_key * flip + x_key * core
                    column = x_key * flip + y_key * core
                    pieces.append(kv[core, g, row, column, which])
            return jnp.concatenate(pieces, axis=0)

        keys = keys_of(0)
        values = keys_of(1)
        at = lax.broadcasted_iota(jnp.int32, (1, HALF), 1)
        y_key = at // GROUP_ROWS
        z_rel = jnp.where(lax.rem(at // SHARD, 2) == 0, select(g, 0), select(g, 1))
        z_key = lax.rem(z + z_rel + DEPTH, DEPTH)
        key_pos = ((last * SIDE + y_key) * 2 + core) * BLOCK + z_key * SHARD + lax.rem(at, SHARD)
        open_width = HALF * last
        start = layer * LAYER_ROWS
        for tile in range(LAYER_ROWS // TILE):
            here = pl.ds(start + tile * TILE, TILE)
            scores = lax.dot_general(
                q_rows[here], keys, (((1,), (1,)), ((), ())), preferred_element_type=jnp.float32
            )
            row = lax.broadcasted_iota(jnp.int32, (TILE, 1), 0) + tile * TILE
            allowed = key_pos <= token_block * BLOCK + row // 2
            edge = jnp.where(allowed, scores[:, open_width:], MASKED)
            pieces = [scores[:, n * HALF : (n + 1) * HALF] for n in range(last)] + [edge]
            peak = functools.reduce(jnp.maximum, pieces)
            old = row_max[here]
            new = jnp.maximum(old, jnp.max(peak, axis=1, keepdims=True))
            fade = jnp.exp2((old - new) * scale2)
            weights = [jnp.exp2((piece - new) * scale2) for piece in pieces]
            row_max[here] = new
            row_sum[here] = row_sum[here] * fade + functools.reduce(jnp.add, weights)
            rounded = jnp.concatenate([w.astype(jnp.bfloat16) for w in weights], axis=1)
            mixed = jnp.dot(rounded, values, preferred_element_type=jnp.float32)
            acc[here] = acc[here] * jnp.concatenate((fade, fade), axis=1) + mixed

    def use(g, rows):
        token_block = place if rows == MINE else place + 1 - 2 * core
        for last in range(SIDE):

            @pl.when(x == last)
            def _(last=last):
                for layer in (2 * rows, 2 * rows + 1):
                    attend(g, layer, token_block, last)

    row_at = lax.broadcasted_iota(jnp.int32, (128, 128), 0)
    diagonal = row_at == lax.broadcasted_iota(jnp.int32, (128, 128), 1)

    def hand_over():
        acc_out[...] = acc[theirs].astype(jnp.bfloat16)
        acc_across.start()
        count = ROWS // 128
        for block in range(count):
            there = pl.ds(ROWS + block * 128, 128)
            total = jnp.sum(row_sum[there], axis=1, keepdims=True)
            for n, value in ((block, row_max[there]), (count + block, total)):
                stat_out[n : n + 1] = jnp.sum(
                    jnp.where(diagonal, value, 0.0), axis=0, keepdims=True
                )
        stat_across.start()

    def drain(g):
        for way in (0, 1):
            own(g, way).wait_send()
            a_on(g, way).wait_send()
            row_out(g, way).wait_send()
            b_on(g, way).wait_send()

    stages = (
        (OFF_OWN, stage_own),
        (OFF_B1, stage_b1),
        (OFF_A1, stage_a1),
        (OFF_B2, stage_b2),
        (OFF_A2, stage_a2),
    )

    def pick(index, table):
        value = jnp.int32(0)
        for n, entry in enumerate(table):
            value = jnp.where(index == n, entry, value)
        return value

    begins = [sum(tick < at for tick, _, _ in ITEMS) for at in range(TICKS + 1)]

    @pl.loop(0, TICKS)
    def _(tick):
        @pl.loop(pick(tick, begins), pick(tick + 1, begins))
        def _(item):
            @pl.when(item == 0)
            def _():
                q_across.wait_recv()

            for n, (_, group, _) in enumerate(HOPS):

                @pl.when(item == ITEMS.index((10, group, SIBLING)))
                def _(n=n):
                    hop(n)[1].wait_recv()

            @pl.when(item == HAND_OVER)
            def _():
                hand_over()

            group = pick(item, [group for _, group, _ in ITEMS])
            rows = pick(item, [rows for _, _, rows in ITEMS])
            for choice in (MINE, SIBLING):

                @pl.when(rows == choice)
                def _(choice=choice):
                    use(group, choice)

        for offset, stage in stages:
            g = tick - offset

            @pl.when((g >= 0) & (g < GROUPS))
            def _(stage=stage, g=g):
                stage(g)

        for step in range(4):

            @pl.when(tick == step)
            def _(step=step):
                prepare(step)

    for move in arrivals.values():
        move.wait_send()
    for n in range(len(HOPS)):
        hop(n)[1].wait_send()
    q_across.wait_send()

    @pl.loop(0, GROUPS)
    def _(g):
        drain(g)

    stat_across.wait()
    acc_across.wait()
    count = ROWS // 128
    for layer, o_ref in enumerate((o1_ref, o2_ref)):
        for part in range(LAYER_ROWS // 128):
            block = layer * (LAYER_ROWS // 128) + part
            here = pl.ds(block * 128, 128)

            def column(n):
                return jnp.sum(jnp.where(diagonal, stat_in[n : n + 1], 0.0), axis=1, keepdims=True)

            own_max, other_max = row_max[here][:, :1], column(block)
            peak = jnp.maximum(own_max, other_max)
            keep = jnp.exp2((own_max - peak) * scale2)
            add = jnp.exp2((other_max - peak) * scale2)
            total = jnp.sum(row_sum[here], axis=1, keepdims=True) * keep + column(count + block) * add
            inverse = 1.0 / total
            result = acc[here] * (keep * inverse) + acc_in[here].astype(jnp.float32) * (add * inverse)
            o_ref[part * 128 : (part + 1) * 128] = result.astype(jnp.bfloat16)


def on_device(queries_first, queries_second, shared_keys, shared_values):
    tokens_here, heads, width = queries_first.shape
    rows = 2 * tokens_here * heads
    scale2 = math.log2(math.e) / math.sqrt(width)
    dma = pltpu.SemaphoreType.DMA
    out = jax.ShapeDtypeStruct((rows // 2, width), jnp.bfloat16)
    vmem = pl.BlockSpec(memory_space=pltpu.VMEM)
    result = pl.pallas_call(
        functools.partial(attention_kernel, scale2),
        out_shape=(out, out),
        in_specs=[pl.BlockSpec(memory_space=pl.ANY)] * 4,
        out_specs=(vmem, vmem),
        scratch_shapes=[
            pltpu.VMEM((2, len(RELATIVE), SIDE, SIDE, 2, GROUP_ROWS, width), jnp.bfloat16),
            pltpu.VMEM((2, tokens_here, heads, width), jnp.bfloat16),
            pltpu.VMEM((2 * rows, width), jnp.bfloat16),
            pltpu.VMEM((2 * rows, 128), jnp.float32),
            pltpu.VMEM((2 * rows, 128), jnp.float32),
            pltpu.VMEM((2 * rows, width), jnp.float32),
            pltpu.VMEM((rows, width), jnp.bfloat16),
            pltpu.VMEM((rows, width), jnp.bfloat16),
            pltpu.VMEM((2 * rows // 128, 128), jnp.float32),
            pltpu.VMEM((2 * rows // 128, 128), jnp.float32),
            dma((4,)),
            dma((GROUPS, 2)),
            dma((GROUPS, 2)),
            dma((4, GROUPS)),
            dma((4, GROUPS)),
            dma((4, GROUPS)),
            dma((4, GROUPS)),
            dma((3,)),
            dma((3,)),
            dma((len(HOPS),)),
            dma((len(HOPS),)),
        ],
        compiler_params=pltpu.CompilerParams(
            collective_id=0, has_side_effects=True, vmem_limit_bytes=56 * 1024 * 1024
        ),
        cost_estimate=pl.CostEstimate(
            flops=4 * rows * 8192 * width, bytes_accessed=1 << 20, transcendentals=rows * 8192
        ),
    )(queries_first, queries_second, shared_keys, shared_values)
    return tuple(array.reshape(tokens_here, heads, width) for array in result)


def solution(mesh):
    return jax.shard_map(
        on_device,
        mesh=mesh,
        in_specs=(
            P("inner", "outer", None),
            P("inner", "outer", None),
            P(("inner", "outer"), None),
            P(("inner", "outer"), None),
        ),
        out_specs=(P("inner", "outer", None), P("inner", "outer", None)),
        check_vma=False,
    )
```

```python
import functools
import math

import jax
import jax.numpy as jnp
from jax import lax
from jax.experimental import pallas as pl
from jax.experimental.pallas import tpu as pltpu
from jax.sharding import PartitionSpec as P

MESH = pl.DeviceIdType.MESH
MASKED = -1e30
FLOOR = -1e20
SIDE = 4
DEPTH = 16
SHARD = 16
GROUP_ROWS = 2 * SHARD
BLOCK = DEPTH * SHARD
HALF = SIDE * GROUP_ROWS
LAYER_ROWS = 2 * BLOCK
ROWS = 2 * LAYER_ROWS
WIDTH = 256
ROUND = ((0, 1), (3, -3), (5, -5), (7, -7), (-1, 2), (-2, 8))
HOPPED = ((4, -4), (6, -6))
RELATIVE = ROUND + HOPPED
GROUPS = len(ROUND)
HOPS = tuple(
    (which, group, half)
    for group in range(GROUPS, len(RELATIVE))
    for which in (0, 1)
    for half in (0, 1)
)
ONWARD = ((1, -2, 3), (-1, 2, -3), (3, -2, 5), (-3, 2, -5), (5, -2, 7), (-5, 2, -7), (7, -1, 8))
OFF_OWN, OFF_A1, OFF_A2, OFF_B1, OFF_B2 = 0, 1, 2, 4, 5
TICKS = GROUPS + OFF_B2 + 1
MINE, SIBLING = 0, 1
ITEMS = (
    (6, 0, SIBLING),
    (7, 1, SIBLING),
    (7, 0, MINE),
    (8, 2, SIBLING),
    (8, 1, MINE),
    (9, 3, SIBLING),
    (9, 2, MINE),
    (10, 4, SIBLING),
    (10, 3, MINE),
    (10, 6, SIBLING),
    (10, 4, MINE),
    (10, 6, MINE),
    (10, 7, SIBLING),
    (11, 5, SIBLING),
    (11, 7, MINE),
    (11, 5, MINE),
)
HAND_OVER = 14
TILE = 256


def place_of(relative):
    for group, members in enumerate(RELATIVE):
        for half, member in enumerate(members):
            if member % DEPTH == relative % DEPTH:
                return group, half
    return None


def attention_kernel(
    scale2,
    q1_hbm,
    q2_hbm,
    k_hbm,
    v_hbm,
    o_ref,
    kv,
    q_in,
    q_rows,
    row_max,
    row_sum,
    acc,
    acc_out,
    acc_in,
    stat_out,
    stat_in,
    in_sem,
    z_send,
    z_recv,
    a_send,
    a_recv,
    b_send,
    b_recv,
    pair_send,
    pair_recv,
    hop_send,
    hop_recv,
):
    z = lax.axis_index("outer")
    place = lax.axis_index("inner")
    core = lax.rem(place, 2)
    chip = place // 2
    x = chip // SIDE
    y = lax.rem(chip, SIDE)
    flip = 1 - core
    a = x * flip + y * core
    b = y * flip + x * core

    def shift(value, by, size):
        return lax.rem(value + by + size, size)

    def inner_of(a_place, b_place):
        x_place = a_place * flip + b_place * core
        y_place = b_place * flip + a_place * core
        return (x_place * SIDE + y_place) * 2 + core

    along_z = {by: (shift(z, by, DEPTH), place) for by in (-2, -1, 1, 2)}
    dev_ap = (z, inner_of(shift(a, 1, SIDE), b))
    dev_am = (z, inner_of(shift(a, -1, SIDE), b))
    dev_bp = (z, inner_of(a, shift(b, 1, SIDE)))
    dev_bm = (z, inner_of(a, shift(b, -1, SIDE)))
    dev_sib = (z, place + 1 - 2 * core)
    am, ap = shift(a, -1, SIDE), shift(a, 1, SIDE)
    bm, bp, bo = shift(b, -1, SIDE), shift(b, 1, SIDE), shift(b, 2, SIDE)

    first_copies = [
        pltpu.make_async_copy(k_hbm, kv.at[core, 0, b, a, 0, pl.ds(0, SHARD)], in_sem.at[0]),
        pltpu.make_async_copy(v_hbm, kv.at[core, 0, b, a, 1, pl.ds(0, SHARD)], in_sem.at[1]),
    ]
    q_copies = [
        pltpu.make_async_copy(source, q_in.at[n], in_sem.at[2 + n])
        for n, source in enumerate((q1_hbm, q2_hbm))
    ]
    for copy in first_copies + q_copies:
        copy.start()

    barrier = pltpu.get_barrier_semaphore()
    for device in (*along_z.values(), dev_ap, dev_am, dev_bp, dev_bm, dev_sib):
        pl.semaphore_signal(barrier, inc=1, device_id=device, device_id_type=MESH)
    for copy in first_copies:
        copy.wait()
    pl.semaphore_wait(barrier, 9)

    def remote(src, dst, send, recv, device):
        return pltpu.make_async_remote_copy(
            src_ref=src,
            dst_ref=dst,
            send_sem=send,
            recv_sem=recv,
            device_id=device,
            device_id_type=MESH,
        )

    def shard(g, half):
        return kv.at[core, g, b, a, :, pl.ds(half * SHARD, SHARD)]

    def z_move(source, by, target):
        g, half = place_of(target)
        return remote(
            shard(*place_of(source)), shard(g, half), z_send.at[g, half], z_recv.at[g, half], along_z[by]
        )

    starts = [z_move(0, -by, by) for by in (1, -1, 2, -2)]
    onward = {source: z_move(source, by, target) for source, by, target in ONWARD}
    arrivals = {target: move for move, target in zip(starts, (1, -1, 2, -2))}
    arrivals.update({target: onward[source] for source, _, target in ONWARD})

    def own(g, way):
        piece = kv.at[core, g, b, a]
        return remote(piece, piece, a_send.at[way, g], a_recv.at[way, g], (dev_ap, dev_am)[way])

    def a_on(g, way):
        piece = kv.at[core, g, b, (am, ap)[way], way]
        return remote(piece, piece, a_send.at[2 + way, g], a_recv.at[2 + way, g], (dev_ap, dev_am)[way])

    def row_out(g, way):
        piece = kv.at[core, g, b]
        return remote(piece, piece, b_send.at[way, g], b_recv.at[way, g], (dev_bp, dev_bm)[way])

    def b_on(g, way):
        piece = kv.at[core, g, (bm, bp)[way], :, way]
        return remote(piece, piece, b_send.at[2 + way, g], b_recv.at[2 + way, g], (dev_bp, dev_bm)[way])

    mine, theirs = pl.ds(0, ROWS), pl.ds(ROWS, ROWS)
    q_across = remote(q_rows.at[mine], q_rows.at[theirs], pair_send.at[0], pair_recv.at[0], dev_sib)
    acc_across = remote(acc_out, acc_in, pair_send.at[1], pair_recv.at[1], dev_sib)
    stat_across = remote(stat_out, stat_in, pair_send.at[2], pair_recv.at[2], dev_sib)

    def hop(n):
        which, group, half = HOPS[n]
        member = RELATIVE[group][half]
        source_group, source_half = place_of(member - 1 if which == 0 else member + 1)
        source = kv.at[core, source_group, :, :, which, pl.ds(source_half * SHARD, SHARD)]
        target = kv.at[core, group, :, :, which, pl.ds(half * SHARD, SHARD)]
        device = along_z[-1 if which == 0 else 1]
        return source_group, remote(source, target, hop_send.at[n], hop_recv.at[n], device)

    for move in starts:
        move.start()

    def stage_own(g):
        for group, members in enumerate(ROUND):

            @pl.when(g == group)
            def _(group=group, members=members):
                waited = (1, -1) if group == 0 else tuple(m for m in members if m != -1)
                for member in waited:
                    arrivals[member].wait_recv()
                    if member in onward:
                        onward[member].start()

        own(g, 0).start()
        own(g, 1).start()

    def stage_a1(g):
        for way in (0, 1):
            own(g, way).wait_recv()
            a_on(g, way).start()

    def stage_a2(g):
        for way in (0, 1):
            a_on(g, way).wait_recv()
        for way in (0, 1):
            row_out(g, way).start()

    def stage_b1(g):
        for way in (0, 1):
            row_out(g, way).wait_recv()
            b_on(g, way).start()

    def stage_b2(g):
        for way in (0, 1):
            b_on(g, way).wait_recv()
        for n in range(len(HOPS)):
            source_group, copy = hop(n)

            @pl.when(g == source_group)
            def _(copy=copy):
                copy.start()

    def select(g, half):
        value = jnp.int32(0)
        for group, members in enumerate(RELATIVE):
            value = jnp.where(g == group, members[half], value)
        return value

    def prepare(step):
        if step < 2:
            q_copies[step].wait()
            q_rows[step * LAYER_ROWS : (step + 1) * LAYER_ROWS] = q_in[step].reshape(LAYER_ROWS, WIDTH)
            if step == 1:
                q_across.start()
        else:
            part = pl.ds((step - 2) * ROWS, ROWS)
            acc[part] = jnp.zeros((ROWS, WIDTH), jnp.float32)
            row_max[part] = jnp.full((ROWS, 128), FLOOR, jnp.float32)
            row_sum[part] = jnp.zeros((ROWS, 128), jnp.float32)

    def attend(g, rows, token_block, last):
        def keys_of(which):
            pieces = []
            for x_key in range(last + 1):
                for y_key in range(SIDE):
                    row = y_key * flip + x_key * core
                    column = x_key * flip + y_key * core
                    pieces.append(kv[core, g, row, column, which])
            return jnp.concatenate(pieces, axis=0)

        keys = keys_of(0)
        values = keys_of(1)
        at = lax.broadcasted_iota(jnp.int32, (1, HALF), 1)
        y_key = at // GROUP_ROWS
        z_rel = jnp.where(lax.rem(at // SHARD, 2) == 0, select(g, 0), select(g, 1))
        z_key = lax.rem(z + z_rel + DEPTH, DEPTH)
        key_pos = ((last * SIDE + y_key) * 2 + core) * BLOCK + z_key * SHARD + lax.rem(at, SHARD)
        open_width = HALF * last
        tiles = [pl.ds(rows * ROWS + n * TILE, TILE) for n in range(ROWS // TILE)]
        scores, weights, fades = {}, {}, {}

        def score_tile(n):
            scores[n] = lax.dot_general(
                q_rows[tiles[n]], keys, (((1,), (1,)), ((), ())), preferred_element_type=jnp.float32
            )

        def soften_tile(n):
            here = tiles[n]
            tile_scores = scores.pop(n)
            row = lax.broadcasted_iota(jnp.int32, (TILE, 1), 0) + (n * TILE) % LAYER_ROWS
            allowed = key_pos <= token_block * BLOCK + row // 2
            edge = jnp.where(allowed, tile_scores[:, open_width:], MASKED)
            pieces = [tile_scores[:, i * HALF : (i + 1) * HALF] for i in range(last)] + [edge]
            peak = functools.reduce(jnp.maximum, pieces)
            old = row_max[here]
            new = jnp.maximum(old, jnp.max(peak, axis=1, keepdims=True))
            fade = jnp.exp2((old - new) * scale2)
            parts = [jnp.exp2((piece - new) * scale2) for piece in pieces]
            row_max[here] = new
            row_sum[here] = row_sum[here] * fade + functools.reduce(jnp.add, parts)
            weights[n] = jnp.concatenate([part.astype(jnp.bfloat16) for part in parts], axis=1)
            fades[n] = fade

        def mix_tile(n):
            here = tiles[n]
            mixed = jnp.dot(weights.pop(n), values, preferred_element_type=jnp.float32)
            acc[here] = acc[here] * jnp.concatenate((fades[n], fades[n]), axis=1) + mixed

        score_tile(0)
        for n in range(len(tiles)):
            if n + 1 < len(tiles):
                score_tile(n + 1)
            if n:
                mix_tile(n - 1)
            soften_tile(n)
        mix_tile(len(tiles) - 1)

    def use(g, rows):
        token_block = place if rows == MINE else place + 1 - 2 * core
        for last in range(SIDE):

            @pl.when(x == last)
            def _(last=last):
                attend(g, rows, token_block, last)

    row_at = lax.broadcasted_iota(jnp.int32, (128, 128), 0)
    diagonal = row_at == lax.broadcasted_iota(jnp.int32, (128, 128), 1)

    def hand_over():
        acc_out[...] = acc[theirs].astype(jnp.bfloat16)
        acc_across.start()
        count = ROWS // 128
        for block in range(count):
            there = pl.ds(ROWS + block * 128, 128)
            total = jnp.sum(row_sum[there], axis=1, keepdims=True)
            for n, value in ((block, row_max[there]), (count + block, total)):
                stat_out[n : n + 1] = jnp.sum(
                    jnp.where(diagonal, value, 0.0), axis=0, keepdims=True
                )
        stat_across.start()

    def drain(g):
        for way in (0, 1):
            own(g, way).wait_send()
            a_on(g, way).wait_send()
            row_out(g, way).wait_send()
            b_on(g, way).wait_send()

    stages = (
        (OFF_OWN, stage_own),
        (OFF_B1, stage_b1),
        (OFF_A1, stage_a1),
        (OFF_B2, stage_b2),
        (OFF_A2, stage_a2),
    )

    def pick(index, table):
        value = jnp.int32(0)
        for n, entry in enumerate(table):
            value = jnp.where(index == n, entry, value)
        return value

    begins = [sum(tick < at for tick, _, _ in ITEMS) for at in range(TICKS + 1)]

    @pl.loop(0, TICKS)
    def _(tick):
        @pl.loop(pick(tick, begins), pick(tick + 1, begins))
        def _(item):
            @pl.when(item == 0)
            def _():
                q_across.wait_recv()

            for n, (_, group, _) in enumerate(HOPS):

                @pl.when(item == ITEMS.index((10, group, SIBLING)))
                def _(n=n):
                    hop(n)[1].wait_recv()

            @pl.when(item == HAND_OVER)
            def _():
                hand_over()

            group = pick(item, [group for _, group, _ in ITEMS])
            rows = pick(item, [rows for _, _, rows in ITEMS])
            for choice in (MINE, SIBLING):

                @pl.when(rows == choice)
                def _(choice=choice):
                    use(group, choice)

        for offset, stage in stages:
            g = tick - offset

            @pl.when((g >= 0) & (g < GROUPS))
            def _(stage=stage, g=g):
                stage(g)

        for step in range(4):

            @pl.when(tick == step)
            def _(step=step):
                prepare(step)

    for move in arrivals.values():
        move.wait_send()
    for n in range(len(HOPS)):
        hop(n)[1].wait_send()
    q_across.wait_send()

    @pl.loop(0, GROUPS)
    def _(g):
        drain(g)

    stat_across.wait()
    acc_across.wait()
    count = ROWS // 128
    for layer in range(2):
        for part in range(LAYER_ROWS // 128):
            block = layer * (LAYER_ROWS // 128) + part
            here = pl.ds(block * 128, 128)

            def column(n):
                return jnp.sum(jnp.where(diagonal, stat_in[n : n + 1], 0.0), axis=1, keepdims=True)

            own_max, other_max = row_max[here][:, :1], column(block)
            peak = jnp.maximum(own_max, other_max)
            keep = jnp.exp2((own_max - peak) * scale2)
            add = jnp.exp2((other_max - peak) * scale2)
            total = jnp.sum(row_sum[here], axis=1, keepdims=True) * keep + column(count + block) * add
            inverse = 1.0 / total
            result = acc[here] * (keep * inverse) + acc_in[here].astype(jnp.float32) * (add * inverse)
            tokens = slice(part * 64, (part + 1) * 64)
            o_ref[tokens, 2 * layer : 2 * layer + 2] = result.astype(jnp.bfloat16).reshape(64, 2, WIDTH)


def on_device(queries_first, queries_second, shared_keys, shared_values):
    tokens_here, heads, width = queries_first.shape
    rows = 2 * tokens_here * heads
    scale2 = math.log2(math.e) / math.sqrt(width)
    dma = pltpu.SemaphoreType.DMA
    out = jax.ShapeDtypeStruct((tokens_here, 2 * heads, width), jnp.bfloat16)
    vmem = pl.BlockSpec(memory_space=pltpu.VMEM)
    result = pl.pallas_call(
        functools.partial(attention_kernel, scale2),
        out_shape=out,
        in_specs=[pl.BlockSpec(memory_space=pl.ANY)] * 4,
        out_specs=vmem,
        scratch_shapes=[
            pltpu.VMEM((2, len(RELATIVE), SIDE, SIDE, 2, GROUP_ROWS, width), jnp.bfloat16),
            pltpu.VMEM((2, tokens_here, heads, width), jnp.bfloat16),
            pltpu.VMEM((2 * rows, width), jnp.bfloat16),
            pltpu.VMEM((2 * rows, 128), jnp.float32),
            pltpu.VMEM((2 * rows, 128), jnp.float32),
            pltpu.VMEM((2 * rows, width), jnp.float32),
            pltpu.VMEM((rows, width), jnp.bfloat16),
            pltpu.VMEM((rows, width), jnp.bfloat16),
            pltpu.VMEM((2 * rows // 128, 128), jnp.float32),
            pltpu.VMEM((2 * rows // 128, 128), jnp.float32),
            dma((4,)),
            dma((GROUPS, 2)),
            dma((GROUPS, 2)),
            dma((4, GROUPS)),
            dma((4, GROUPS)),
            dma((4, GROUPS)),
            dma((4, GROUPS)),
            dma((3,)),
            dma((3,)),
            dma((len(HOPS),)),
            dma((len(HOPS),)),
        ],
        compiler_params=pltpu.CompilerParams(
            collective_id=0, has_side_effects=True, vmem_limit_bytes=56 * 1024 * 1024
        ),
        cost_estimate=pl.CostEstimate(
            flops=4 * rows * 8192 * width, bytes_accessed=1 << 20, transcendentals=rows * 8192
        ),
    )(queries_first, queries_second, shared_keys, shared_values)
    return result[:, :heads], result[:, heads:]


def solution(mesh):
    return jax.shard_map(
        on_device,
        mesh=mesh,
        in_specs=(
            P("inner", "outer", None),
            P("inner", "outer", None),
            P(("inner", "outer"), None),
            P(("inner", "outer"), None),
        ),
        out_specs=(P("inner", "outer", None), P("inner", "outer", None)),
        check_vma=False,
    )
```

```python
import functools
import math

import jax
import jax.numpy as jnp
from jax import lax
from jax.experimental import pallas as pl
from jax.experimental.pallas import tpu as pltpu
from jax.sharding import PartitionSpec as P

MESH = pl.DeviceIdType.MESH
MASKED = -1e30
FLOOR = -1e20
SIDE = 4
DEPTH = 16
SHARD = 16
GROUP_ROWS = 2 * SHARD
BLOCK = DEPTH * SHARD
HALF = SIDE * GROUP_ROWS
LAYER_ROWS = 2 * BLOCK
ROWS = 2 * LAYER_ROWS
WIDTH = 256
ROUND = ((0, 1), (3, -3), (5, -5), (7, -7), (-1, 2), (-2, 8))
HOPPED = ((4, -4), (6, -6))
RELATIVE = ROUND + HOPPED
GROUPS = len(ROUND)
HOPS = tuple(
    (which, group, half)
    for group in range(GROUPS, len(RELATIVE))
    for which in (0, 1)
    for half in (0, 1)
)
ONWARD = ((1, -2, 3), (-1, 2, -3), (3, -2, 5), (-3, 2, -5), (5, -2, 7), (-5, 2, -7), (7, -1, 8))
OFF_OWN, OFF_A1, OFF_A2, OFF_B1, OFF_B2 = 0, 1, 2, 4, 5
TICKS = GROUPS + OFF_B2 + 1
MINE, SIBLING = 0, 1
ITEMS = (
    (6, 0, SIBLING),
    (6, 0, MINE),
    (7, 1, SIBLING),
    (7, 1, MINE),
    (8, 2, SIBLING),
    (8, 2, MINE),
    (9, 3, SIBLING),
    (9, 3, MINE),
    (9, 6, SIBLING),
    (9, 6, MINE),
    (10, 4, SIBLING),
    (10, 7, SIBLING),
    (10, 4, MINE),
    (11, 5, SIBLING),
    (11, 7, MINE),
    (11, 5, MINE),
)
HAND_OVER = 14
TILE = 256


def place_of(relative):
    for group, members in enumerate(RELATIVE):
        for half, member in enumerate(members):
            if member % DEPTH == relative % DEPTH:
                return group, half
    return None


def attention_kernel(
    scale2,
    q1_hbm,
    q2_hbm,
    k_hbm,
    v_hbm,
    o_ref,
    kv,
    q_in,
    q_rows,
    row_max,
    row_sum,
    acc,
    acc_out,
    acc_in,
    stat_out,
    stat_in,
    in_sem,
    z_send,
    z_recv,
    a_send,
    a_recv,
    b_send,
    b_recv,
    pair_send,
    pair_recv,
    hop_send,
    hop_recv,
):
    z = lax.axis_index("outer")
    place = lax.axis_index("inner")
    core = lax.rem(place, 2)
    chip = place // 2
    x = chip // SIDE
    y = lax.rem(chip, SIDE)
    flip = 1 - core
    a = x * flip + y * core
    b = y * flip + x * core

    def shift(value, by, size):
        return lax.rem(value + by + size, size)

    def inner_of(a_place, b_place):
        x_place = a_place * flip + b_place * core
        y_place = b_place * flip + a_place * core
        return (x_place * SIDE + y_place) * 2 + core

    along_z = {by: (shift(z, by, DEPTH), place) for by in (-2, -1, 1, 2)}
    dev_ap = (z, inner_of(shift(a, 1, SIDE), b))
    dev_am = (z, inner_of(shift(a, -1, SIDE), b))
    dev_bp = (z, inner_of(a, shift(b, 1, SIDE)))
    dev_bm = (z, inner_of(a, shift(b, -1, SIDE)))
    dev_sib = (z, place + 1 - 2 * core)
    am, ap = shift(a, -1, SIDE), shift(a, 1, SIDE)
    bm, bp, bo = shift(b, -1, SIDE), shift(b, 1, SIDE), shift(b, 2, SIDE)

    first_copies = [
        pltpu.make_async_copy(k_hbm, kv.at[core, 0, b, a, 0, pl.ds(0, SHARD)], in_sem.at[0]),
        pltpu.make_async_copy(v_hbm, kv.at[core, 0, b, a, 1, pl.ds(0, SHARD)], in_sem.at[1]),
    ]
    q_copies = [
        pltpu.make_async_copy(source, q_in.at[n], in_sem.at[2 + n])
        for n, source in enumerate((q1_hbm, q2_hbm))
    ]
    for copy in first_copies + q_copies:
        copy.start()

    barrier = pltpu.get_barrier_semaphore()
    for device in (*along_z.values(), dev_ap, dev_am, dev_bp, dev_bm, dev_sib):
        pl.semaphore_signal(barrier, inc=1, device_id=device, device_id_type=MESH)
    for copy in first_copies:
        copy.wait()
    pl.semaphore_wait(barrier, 9)

    def remote(src, dst, send, recv, device):
        return pltpu.make_async_remote_copy(
            src_ref=src,
            dst_ref=dst,
            send_sem=send,
            recv_sem=recv,
            device_id=device,
            device_id_type=MESH,
        )

    def shard(g, half):
        return kv.at[core, g, b, a, :, pl.ds(half * SHARD, SHARD)]

    def z_move(source, by, target):
        g, half = place_of(target)
        return remote(
            shard(*place_of(source)), shard(g, half), z_send.at[g, half], z_recv.at[g, half], along_z[by]
        )

    starts = [z_move(0, -by, by) for by in (1, -1, 2, -2)]
    onward = {source: z_move(source, by, target) for source, by, target in ONWARD}
    arrivals = {target: move for move, target in zip(starts, (1, -1, 2, -2))}
    arrivals.update({target: onward[source] for source, _, target in ONWARD})

    def own(g, way):
        piece = kv.at[core, g, b, a]
        return remote(piece, piece, a_send.at[way, g], a_recv.at[way, g], (dev_ap, dev_am)[way])

    def a_on(g, way):
        piece = kv.at[core, g, b, (am, ap)[way], way]
        return remote(piece, piece, a_send.at[2 + way, g], a_recv.at[2 + way, g], (dev_ap, dev_am)[way])

    def row_out(g, way):
        piece = kv.at[core, g, b]
        return remote(piece, piece, b_send.at[way, g], b_recv.at[way, g], (dev_bp, dev_bm)[way])

    def b_on(g, way):
        piece = kv.at[core, g, (bm, bp)[way], :, way]
        return remote(piece, piece, b_send.at[2 + way, g], b_recv.at[2 + way, g], (dev_bp, dev_bm)[way])

    mine, theirs = pl.ds(0, ROWS), pl.ds(ROWS, ROWS)
    q_across = remote(q_rows.at[mine], q_rows.at[theirs], pair_send.at[0], pair_recv.at[0], dev_sib)
    acc_across = remote(acc_out, acc_in, pair_send.at[1], pair_recv.at[1], dev_sib)
    stat_across = remote(stat_out, stat_in, pair_send.at[2], pair_recv.at[2], dev_sib)

    def hop(n):
        which, group, half = HOPS[n]
        member = RELATIVE[group][half]
        source_group, source_half = place_of(member - 1 if which == 0 else member + 1)
        source = kv.at[core, source_group, :, :, which, pl.ds(source_half * SHARD, SHARD)]
        target = kv.at[core, group, :, :, which, pl.ds(half * SHARD, SHARD)]
        device = along_z[-1 if which == 0 else 1]
        return source_group, remote(source, target, hop_send.at[n], hop_recv.at[n], device)

    for move in starts:
        move.start()

    def stage_own(g):
        for group, members in enumerate(ROUND):

            @pl.when(g == group)
            def _(group=group, members=members):
                waited = (1, -1) if group == 0 else tuple(m for m in members if m != -1)
                for member in waited:
                    arrivals[member].wait_recv()
                    if member in onward:
                        onward[member].start()

        own(g, 0).start()
        own(g, 1).start()

    def stage_a1(g):
        for way in (0, 1):
            own(g, way).wait_recv()
            a_on(g, way).start()

    def stage_a2(g):
        for way in (0, 1):
            a_on(g, way).wait_recv()
        for way in (0, 1):
            row_out(g, way).start()

    def stage_b1(g):
        for way in (0, 1):
            row_out(g, way).wait_recv()
            b_on(g, way).start()

    def stage_b2(g):
        for way in (0, 1):
            b_on(g, way).wait_recv()
        for n in range(len(HOPS)):
            source_group, copy = hop(n)

            @pl.when(g == source_group)
            def _(copy=copy):
                copy.start()

    def select(g, half):
        value = jnp.int32(0)
        for group, members in enumerate(RELATIVE):
            value = jnp.where(g == group, members[half], value)
        return value

    def prepare(step):
        if step < 2:
            q_copies[step].wait()
            q_rows[step * LAYER_ROWS : (step + 1) * LAYER_ROWS] = q_in[step].reshape(LAYER_ROWS, WIDTH)
            if step == 1:
                q_across.start()
        else:
            part = pl.ds((step - 2) * ROWS, ROWS)
            acc[part] = jnp.zeros((ROWS, WIDTH), jnp.float32)
            row_max[part] = jnp.full((ROWS, 128), FLOOR, jnp.float32)
            row_sum[part] = jnp.zeros((ROWS, 128), jnp.float32)

    def attend(g, rows, token_block, last):
        def keys_of(which):
            pieces = []
            for x_key in range(last + 1):
                for y_key in range(SIDE):
                    row = y_key * flip + x_key * core
                    column = x_key * flip + y_key * core
                    pieces.append(kv[core, g, row, column, which])
            return jnp.concatenate(pieces, axis=0)

        keys = keys_of(0)
        values = keys_of(1)
        at = lax.broadcasted_iota(jnp.int32, (1, HALF), 1)
        y_key = at // GROUP_ROWS
        z_rel = jnp.where(lax.rem(at // SHARD, 2) == 0, select(g, 0), select(g, 1))
        z_key = lax.rem(z + z_rel + DEPTH, DEPTH)
        key_pos = ((last * SIDE + y_key) * 2 + core) * BLOCK + z_key * SHARD + lax.rem(at, SHARD)
        open_width = HALF * last
        tiles = [pl.ds(rows * ROWS + n * TILE, TILE) for n in range(ROWS // TILE)]
        scores, weights, fades = {}, {}, {}

        def score_tile(n):
            scores[n] = lax.dot_general(
                q_rows[tiles[n]], keys, (((1,), (1,)), ((), ())), preferred_element_type=jnp.float32
            )

        def soften_tile(n):
            here = tiles[n]
            tile_scores = scores.pop(n)
            row = lax.broadcasted_iota(jnp.int32, (TILE, 1), 0) + (n * TILE) % LAYER_ROWS
            allowed = key_pos <= token_block * BLOCK + row // 2
            edge = jnp.where(allowed, tile_scores[:, open_width:], MASKED)
            pieces = [tile_scores[:, i * HALF : (i + 1) * HALF] for i in range(last)] + [edge]
            peak = functools.reduce(jnp.maximum, pieces)
            old = row_max[here]
            new = jnp.maximum(old, jnp.max(peak, axis=1, keepdims=True))
            fade = jnp.exp2((old - new) * scale2)
            parts = [jnp.exp2((piece - new) * scale2) for piece in pieces]
            row_max[here] = new
            row_sum[here] = row_sum[here] * fade + functools.reduce(jnp.add, parts)
            weights[n] = jnp.concatenate([part.astype(jnp.bfloat16) for part in parts], axis=1)
            fades[n] = fade

        def mix_tile(n):
            here = tiles[n]
            mixed = jnp.dot(weights.pop(n), values, preferred_element_type=jnp.float32)
            acc[here] = acc[here] * jnp.concatenate((fades[n], fades[n]), axis=1) + mixed

        score_tile(0)
        for n in range(len(tiles)):
            if n + 1 < len(tiles):
                score_tile(n + 1)
            if n:
                mix_tile(n - 1)
            soften_tile(n)
        mix_tile(len(tiles) - 1)

    def use(g, rows):
        token_block = place if rows == MINE else place + 1 - 2 * core
        for last in range(SIDE):

            @pl.when(x == last)
            def _(last=last):
                attend(g, rows, token_block, last)

    row_at = lax.broadcasted_iota(jnp.int32, (128, 128), 0)
    diagonal = row_at == lax.broadcasted_iota(jnp.int32, (128, 128), 1)

    def hand_over():
        acc_out[...] = acc[theirs].astype(jnp.bfloat16)
        acc_across.start()
        count = ROWS // 128
        for block in range(count):
            there = pl.ds(ROWS + block * 128, 128)
            total = jnp.sum(row_sum[there], axis=1, keepdims=True)
            for n, value in ((block, row_max[there]), (count + block, total)):
                stat_out[n : n + 1] = jnp.sum(
                    jnp.where(diagonal, value, 0.0), axis=0, keepdims=True
                )
        stat_across.start()

    def drain(g):
        for way in (0, 1):
            own(g, way).wait_send()
            a_on(g, way).wait_send()
            row_out(g, way).wait_send()
            b_on(g, way).wait_send()

    stages = (
        (OFF_OWN, stage_own),
        (OFF_B1, stage_b1),
        (OFF_A1, stage_a1),
        (OFF_B2, stage_b2),
        (OFF_A2, stage_a2),
    )

    def pick(index, table):
        value = jnp.int32(0)
        for n, entry in enumerate(table):
            value = jnp.where(index == n, entry, value)
        return value

    begins = [sum(tick < at for tick, _, _ in ITEMS) for at in range(TICKS + 1)]

    @pl.loop(0, TICKS)
    def _(tick):
        @pl.loop(pick(tick, begins), pick(tick + 1, begins))
        def _(item):
            @pl.when(item == 0)
            def _():
                q_across.wait_recv()

            for n, (_, group, _) in enumerate(HOPS):

                @pl.when(item == ITEMS.index((9 if group == GROUPS else 10, group, SIBLING)))
                def _(n=n):
                    hop(n)[1].wait_recv()

            @pl.when(item == HAND_OVER)
            def _():
                hand_over()

            group = pick(item, [group for _, group, _ in ITEMS])
            rows = pick(item, [rows for _, _, rows in ITEMS])
            for choice in (MINE, SIBLING):

                @pl.when(rows == choice)
                def _(choice=choice):
                    use(group, choice)

        for offset, stage in stages:
            g = tick - offset

            @pl.when((g >= 0) & (g < GROUPS))
            def _(stage=stage, g=g):
                stage(g)

        for step in range(4):

            @pl.when(tick == step)
            def _(step=step):
                prepare(step)

    for move in arrivals.values():
        move.wait_send()
    for n in range(len(HOPS)):
        hop(n)[1].wait_send()
    q_across.wait_send()

    @pl.loop(0, GROUPS)
    def _(g):
        drain(g)

    stat_across.wait()
    acc_across.wait()
    count = ROWS // 128
    for layer in range(2):
        for part in range(LAYER_ROWS // 128):
            block = layer * (LAYER_ROWS // 128) + part
            here = pl.ds(block * 128, 128)

            def column(n):
                return jnp.sum(jnp.where(diagonal, stat_in[n : n + 1], 0.0), axis=1, keepdims=True)

            own_max, other_max = row_max[here][:, :1], column(block)
            peak = jnp.maximum(own_max, other_max)
            keep = jnp.exp2((own_max - peak) * scale2)
            add = jnp.exp2((other_max - peak) * scale2)
            total = jnp.sum(row_sum[here], axis=1, keepdims=True) * keep + column(count + block) * add
            inverse = 1.0 / total
            result = acc[here] * (keep * inverse) + acc_in[here].astype(jnp.float32) * (add * inverse)
            tokens = slice(part * 64, (part + 1) * 64)
            o_ref[tokens, 2 * layer : 2 * layer + 2] = result.astype(jnp.bfloat16).reshape(64, 2, WIDTH)


def on_device(queries_first, queries_second, shared_keys, shared_values):
    tokens_here, heads, width = queries_first.shape
    rows = 2 * tokens_here * heads
    scale2 = math.log2(math.e) / math.sqrt(width)
    dma = pltpu.SemaphoreType.DMA
    out = jax.ShapeDtypeStruct((tokens_here, 2 * heads, width), jnp.bfloat16)
    vmem = pl.BlockSpec(memory_space=pltpu.VMEM)
    result = pl.pallas_call(
        functools.partial(attention_kernel, scale2),
        out_shape=out,
        in_specs=[pl.BlockSpec(memory_space=pl.ANY)] * 4,
        out_specs=vmem,
        scratch_shapes=[
            pltpu.VMEM((2, len(RELATIVE), SIDE, SIDE, 2, GROUP_ROWS, width), jnp.bfloat16),
            pltpu.VMEM((2, tokens_here, heads, width), jnp.bfloat16),
            pltpu.VMEM((2 * rows, width), jnp.bfloat16),
            pltpu.VMEM((2 * rows, 128), jnp.float32),
            pltpu.VMEM((2 * rows, 128), jnp.float32),
            pltpu.VMEM((2 * rows, width), jnp.float32),
            pltpu.VMEM((rows, width), jnp.bfloat16),
            pltpu.VMEM((rows, width), jnp.bfloat16),
            pltpu.VMEM((2 * rows // 128, 128), jnp.float32),
            pltpu.VMEM((2 * rows // 128, 128), jnp.float32),
            dma((4,)),
            dma((GROUPS, 2)),
            dma((GROUPS, 2)),
            dma((4, GROUPS)),
            dma((4, GROUPS)),
            dma((4, GROUPS)),
            dma((4, GROUPS)),
            dma((3,)),
            dma((3,)),
            dma((len(HOPS),)),
            dma((len(HOPS),)),
        ],
        compiler_params=pltpu.CompilerParams(
            collective_id=0, has_side_effects=True, vmem_limit_bytes=56 * 1024 * 1024
        ),
        cost_estimate=pl.CostEstimate(
            flops=4 * rows * 8192 * width, bytes_accessed=1 << 20, transcendentals=rows * 8192
        ),
    )(queries_first, queries_second, shared_keys, shared_values)
    return result[:, :heads], result[:, heads:]


def solution(mesh):
    return jax.shard_map(
        on_device,
        mesh=mesh,
        in_specs=(
            P("inner", "outer", None),
            P("inner", "outer", None),
            P(("inner", "outer"), None),
            P(("inner", "outer"), None),
        ),
        out_specs=(P("inner", "outer", None), P("inner", "outer", None)),
        check_vma=False,
    )
```

```python
import functools
import math

import jax
import jax.numpy as jnp
from jax import lax
from jax.experimental import pallas as pl
from jax.experimental.pallas import tpu as pltpu
from jax.sharding import PartitionSpec as P

MESH = pl.DeviceIdType.MESH
MASKED = -1e30
FLOOR = -1e20
SIDE = 4
DEPTH = 16
SHARD = 16
GROUP_ROWS = 2 * SHARD
BLOCK = DEPTH * SHARD
HALF = SIDE * GROUP_ROWS
LAYER_ROWS = 2 * BLOCK
ROWS = 2 * LAYER_ROWS
WIDTH = 256
ROUND = ((0, 1), (3, -3), (5, -5), (7, -7), (-1, 2), (-2, 8))
HOPPED = ((4, -4), (6, -6))
RELATIVE = ROUND + HOPPED
GROUPS = len(ROUND)
HOPS = tuple(
    (which, group, half)
    for group in range(GROUPS, len(RELATIVE))
    for which in (0, 1)
    for half in (0, 1)
)
ONWARD = ((1, -2, 3), (-1, 2, -3), (3, -2, 5), (-3, 2, -5), (5, -2, 7), (-5, 2, -7), (7, -1, 8))
OFF_OWN, OFF_A1, OFF_A2, OFF_B1, OFF_B2 = 0, 1, 2, 4, 5
TICKS = GROUPS + OFF_B2 + 1
MINE, SIBLING = 0, 1
ITEMS = (
    (6, 0, SIBLING),
    (6, 0, MINE),
    (7, 1, SIBLING),
    (7, 1, MINE),
    (8, 2, SIBLING),
    (8, 2, MINE),
    (9, 3, SIBLING),
    (9, 3, MINE),
    (9, 6, SIBLING),
    (9, 6, MINE),
    (10, 4, SIBLING),
    (10, 4, MINE),
    (10, 7, SIBLING),
    (11, 5, SIBLING),
    (11, 7, MINE),
    (11, 5, MINE),
)
HAND_OVER = 14
TILE = 512


def place_of(relative):
    for group, members in enumerate(RELATIVE):
        for half, member in enumerate(members):
            if member % DEPTH == relative % DEPTH:
                return group, half
    return None


def attention_kernel(
    scale2,
    q1_hbm,
    q2_hbm,
    k_hbm,
    v_hbm,
    o_ref,
    kv,
    q_in,
    q_rows,
    row_max,
    row_sum,
    acc,
    acc_out,
    acc_in,
    stat_out,
    stat_in,
    in_sem,
    z_send,
    z_recv,
    a_send,
    a_recv,
    b_send,
    b_recv,
    pair_send,
    pair_recv,
    hop_send,
    hop_recv,
):
    z = lax.axis_index("outer")
    place = lax.axis_index("inner")
    core = lax.rem(place, 2)
    chip = place // 2
    x = chip // SIDE
    y = lax.rem(chip, SIDE)
    flip = 1 - core
    a = x * flip + y * core
    b = y * flip + x * core

    def shift(value, by, size):
        return lax.rem(value + by + size, size)

    def inner_of(a_place, b_place):
        x_place = a_place * flip + b_place * core
        y_place = b_place * flip + a_place * core
        return (x_place * SIDE + y_place) * 2 + core

    along_z = {by: (shift(z, by, DEPTH), place) for by in (-2, -1, 1, 2)}
    dev_ap = (z, inner_of(shift(a, 1, SIDE), b))
    dev_am = (z, inner_of(shift(a, -1, SIDE), b))
    dev_bp = (z, inner_of(a, shift(b, 1, SIDE)))
    dev_bm = (z, inner_of(a, shift(b, -1, SIDE)))
    dev_sib = (z, place + 1 - 2 * core)
    am, ap = shift(a, -1, SIDE), shift(a, 1, SIDE)
    bm, bp, bo = shift(b, -1, SIDE), shift(b, 1, SIDE), shift(b, 2, SIDE)

    first_copies = [
        pltpu.make_async_copy(k_hbm, kv.at[core, 0, b, a, 0, pl.ds(0, SHARD)], in_sem.at[0]),
        pltpu.make_async_copy(v_hbm, kv.at[core, 0, b, a, 1, pl.ds(0, SHARD)], in_sem.at[1]),
    ]
    q_copies = [
        pltpu.make_async_copy(source, q_in.at[n], in_sem.at[2 + n])
        for n, source in enumerate((q1_hbm, q2_hbm))
    ]
    for copy in first_copies + q_copies:
        copy.start()

    barrier = pltpu.get_barrier_semaphore()
    for device in (*along_z.values(), dev_ap, dev_am, dev_bp, dev_bm, dev_sib):
        pl.semaphore_signal(barrier, inc=1, device_id=device, device_id_type=MESH)
    for copy in first_copies:
        copy.wait()
    pl.semaphore_wait(barrier, 9)

    def remote(src, dst, send, recv, device):
        return pltpu.make_async_remote_copy(
            src_ref=src,
            dst_ref=dst,
            send_sem=send,
            recv_sem=recv,
            device_id=device,
            device_id_type=MESH,
        )

    def shard(g, half):
        return kv.at[core, g, b, a, :, pl.ds(half * SHARD, SHARD)]

    def z_move(source, by, target):
        g, half = place_of(target)
        return remote(
            shard(*place_of(source)), shard(g, half), z_send.at[g, half], z_recv.at[g, half], along_z[by]
        )

    starts = [z_move(0, -by, by) for by in (1, -1, 2, -2)]
    onward = {source: z_move(source, by, target) for source, by, target in ONWARD}
    arrivals = {target: move for move, target in zip(starts, (1, -1, 2, -2))}
    arrivals.update({target: onward[source] for source, _, target in ONWARD})

    def own(g, way):
        piece = kv.at[core, g, b, a]
        return remote(piece, piece, a_send.at[way, g], a_recv.at[way, g], (dev_ap, dev_am)[way])

    def a_on(g, way):
        piece = kv.at[core, g, b, (am, ap)[way], way]
        return remote(piece, piece, a_send.at[2 + way, g], a_recv.at[2 + way, g], (dev_ap, dev_am)[way])

    def row_out(g, way):
        piece = kv.at[core, g, b]
        return remote(piece, piece, b_send.at[way, g], b_recv.at[way, g], (dev_bp, dev_bm)[way])

    def b_on(g, way):
        piece = kv.at[core, g, (bm, bp)[way], :, way]
        return remote(piece, piece, b_send.at[2 + way, g], b_recv.at[2 + way, g], (dev_bp, dev_bm)[way])

    mine, theirs = pl.ds(0, ROWS), pl.ds(ROWS, ROWS)
    q_across = remote(q_rows.at[mine], q_rows.at[theirs], pair_send.at[0], pair_recv.at[0], dev_sib)
    acc_across = remote(acc_out, acc_in, pair_send.at[1], pair_recv.at[1], dev_sib)
    stat_across = remote(stat_out, stat_in, pair_send.at[2], pair_recv.at[2], dev_sib)

    def hop(n):
        which, group, half = HOPS[n]
        member = RELATIVE[group][half]
        source_group, source_half = place_of(member - 1 if which == 0 else member + 1)
        source = kv.at[core, source_group, :, :, which, pl.ds(source_half * SHARD, SHARD)]
        target = kv.at[core, group, :, :, which, pl.ds(half * SHARD, SHARD)]
        device = along_z[-1 if which == 0 else 1]
        return source_group, remote(source, target, hop_send.at[n], hop_recv.at[n], device)

    for move in starts:
        move.start()

    def stage_own(g):
        for group, members in enumerate(ROUND):

            @pl.when(g == group)
            def _(group=group, members=members):
                waited = (1, -1) if group == 0 else tuple(m for m in members if m != -1)
                for member in waited:
                    arrivals[member].wait_recv()
                    if member in onward:
                        onward[member].start()

        own(g, 0).start()
        own(g, 1).start()

    def stage_a1(g):
        for way in (0, 1):
            own(g, way).wait_recv()
            a_on(g, way).start()

    def stage_a2(g):
        for way in (0, 1):
            a_on(g, way).wait_recv()
        for way in (0, 1):
            row_out(g, way).start()

    def stage_b1(g):
        for way in (0, 1):
            row_out(g, way).wait_recv()
            b_on(g, way).start()

    def stage_b2(g):
        for way in (0, 1):
            b_on(g, way).wait_recv()
        for n in range(len(HOPS)):
            source_group, copy = hop(n)

            @pl.when(g == source_group)
            def _(copy=copy):
                copy.start()

    def select(g, half):
        value = jnp.int32(0)
        for group, members in enumerate(RELATIVE):
            value = jnp.where(g == group, members[half], value)
        return value

    def prepare(step):
        if step < 2:
            q_copies[step].wait()
            q_rows[step * LAYER_ROWS : (step + 1) * LAYER_ROWS] = q_in[step].reshape(LAYER_ROWS, WIDTH)
            if step == 1:
                q_across.start()
        else:
            part = pl.ds((step - 2) * ROWS, ROWS)
            acc[part] = jnp.zeros((ROWS, WIDTH), jnp.float32)
            row_max[part] = jnp.full((ROWS, 128), FLOOR, jnp.float32)
            row_sum[part] = jnp.zeros((ROWS, 128), jnp.float32)

    def attend(g, rows, token_block, last):
        def keys_of(which):
            pieces = []
            for x_key in range(last + 1):
                for y_key in range(SIDE):
                    row = y_key * flip + x_key * core
                    column = x_key * flip + y_key * core
                    pieces.append(kv[core, g, row, column, which])
            return jnp.concatenate(pieces, axis=0)

        keys = keys_of(0)
        values = keys_of(1)
        at = lax.broadcasted_iota(jnp.int32, (1, HALF), 1)
        y_key = at // GROUP_ROWS
        z_rel = jnp.where(lax.rem(at // SHARD, 2) == 0, select(g, 0), select(g, 1))
        z_key = lax.rem(z + z_rel + DEPTH, DEPTH)
        key_pos = ((last * SIDE + y_key) * 2 + core) * BLOCK + z_key * SHARD + lax.rem(at, SHARD)
        open_width = HALF * last
        tiles = [pl.ds(rows * ROWS + n * TILE, TILE) for n in range(ROWS // TILE)]
        scores, weights, fades = {}, {}, {}

        def score_tile(n):
            scores[n] = lax.dot_general(
                q_rows[tiles[n]], keys, (((1,), (1,)), ((), ())), preferred_element_type=jnp.float32
            )

        def soften_tile(n):
            here = tiles[n]
            tile_scores = scores.pop(n)
            row = lax.broadcasted_iota(jnp.int32, (TILE, 1), 0) + (n * TILE) % LAYER_ROWS
            allowed = key_pos <= token_block * BLOCK + row // 2
            edge = jnp.where(allowed, tile_scores[:, open_width:], MASKED)
            pieces = [tile_scores[:, i * HALF : (i + 1) * HALF] for i in range(last)] + [edge]
            peak = functools.reduce(jnp.maximum, pieces)
            old = row_max[here]
            new = jnp.maximum(old, jnp.max(peak, axis=1, keepdims=True))
            fade = jnp.exp2((old - new) * scale2)
            parts = [jnp.exp2((piece - new) * scale2) for piece in pieces]
            row_max[here] = new
            row_sum[here] = row_sum[here] * fade + functools.reduce(jnp.add, parts)
            weights[n] = jnp.concatenate([part.astype(jnp.bfloat16) for part in parts], axis=1)
            fades[n] = fade

        def mix_tile(n):
            here = tiles[n]
            mixed = jnp.dot(weights.pop(n), values, preferred_element_type=jnp.float32)
            acc[here] = acc[here] * jnp.concatenate((fades[n], fades[n]), axis=1) + mixed

        score_tile(0)
        for n in range(len(tiles)):
            if n + 1 < len(tiles):
                score_tile(n + 1)
            if n:
                mix_tile(n - 1)
            soften_tile(n)
        mix_tile(len(tiles) - 1)

    def use(g, rows):
        token_block = place if rows == MINE else place + 1 - 2 * core
        for last in range(SIDE):

            @pl.when(x == last)
            def _(last=last):
                attend(g, rows, token_block, last)

    row_at = lax.broadcasted_iota(jnp.int32, (128, 128), 0)
    diagonal = row_at == lax.broadcasted_iota(jnp.int32, (128, 128), 1)

    def hand_over():
        acc_out[...] = acc[theirs].astype(jnp.bfloat16)
        acc_across.start()
        count = ROWS // 128
        for block in range(count):
            there = pl.ds(ROWS + block * 128, 128)
            total = jnp.sum(row_sum[there], axis=1, keepdims=True)
            for n, value in ((block, row_max[there]), (count + block, total)):
                stat_out[n : n + 1] = jnp.sum(
                    jnp.where(diagonal, value, 0.0), axis=0, keepdims=True
                )
        stat_across.start()

    def drain(g):
        for way in (0, 1):
            own(g, way).wait_send()
            a_on(g, way).wait_send()
            row_out(g, way).wait_send()
            b_on(g, way).wait_send()

    stages = (
        (OFF_OWN, stage_own),
        (OFF_B1, stage_b1),
        (OFF_A1, stage_a1),
        (OFF_B2, stage_b2),
        (OFF_A2, stage_a2),
    )

    def pick(index, table):
        value = jnp.int32(0)
        for n, entry in enumerate(table):
            value = jnp.where(index == n, entry, value)
        return value

    begins = [sum(tick < at for tick, _, _ in ITEMS) for at in range(TICKS + 1)]

    @pl.loop(0, TICKS)
    def _(tick):
        @pl.loop(pick(tick, begins), pick(tick + 1, begins))
        def _(item):
            @pl.when(item == 0)
            def _():
                q_across.wait_recv()

            for n, (_, group, _) in enumerate(HOPS):

                @pl.when(item == ITEMS.index((9 if group == GROUPS else 10, group, SIBLING)))
                def _(n=n):
                    hop(n)[1].wait_recv()

            @pl.when(item == HAND_OVER)
            def _():
                hand_over()

            group = pick(item, [group for _, group, _ in ITEMS])
            rows = pick(item, [rows for _, _, rows in ITEMS])
            for choice in (MINE, SIBLING):

                @pl.when(rows == choice)
                def _(choice=choice):
                    use(group, choice)

        for offset, stage in stages:
            g = tick - offset

            @pl.when((g >= 0) & (g < GROUPS))
            def _(stage=stage, g=g):
                stage(g)

        for step in range(4):

            @pl.when(tick == step)
            def _(step=step):
                prepare(step)

    for move in arrivals.values():
        move.wait_send()
    for n in range(len(HOPS)):
        hop(n)[1].wait_send()
    q_across.wait_send()

    @pl.loop(0, GROUPS)
    def _(g):
        drain(g)

    stat_across.wait()
    acc_across.wait()
    count = ROWS // 128
    for layer in range(2):
        for part in range(LAYER_ROWS // 128):
            block = layer * (LAYER_ROWS // 128) + part
            here = pl.ds(block * 128, 128)

            def column(n):
                return jnp.sum(jnp.where(diagonal, stat_in[n : n + 1], 0.0), axis=1, keepdims=True)

            own_max, other_max = row_max[here][:, :1], column(block)
            peak = jnp.maximum(own_max, other_max)
            keep = jnp.exp2((own_max - peak) * scale2)
            add = jnp.exp2((other_max - peak) * scale2)
            total = jnp.sum(row_sum[here], axis=1, keepdims=True) * keep + column(count + block) * add
            inverse = 1.0 / total
            result = acc[here] * (keep * inverse) + acc_in[here].astype(jnp.float32) * (add * inverse)
            tokens = slice(part * 64, (part + 1) * 64)
            o_ref[tokens, 2 * layer : 2 * layer + 2] = result.astype(jnp.bfloat16).reshape(64, 2, WIDTH)


def on_device(queries_first, queries_second, shared_keys, shared_values):
    tokens_here, heads, width = queries_first.shape
    rows = 2 * tokens_here * heads
    scale2 = math.log2(math.e) / math.sqrt(width)
    dma = pltpu.SemaphoreType.DMA
    out = jax.ShapeDtypeStruct((tokens_here, 2 * heads, width), jnp.bfloat16)
    vmem = pl.BlockSpec(memory_space=pltpu.VMEM)
    result = pl.pallas_call(
        functools.partial(attention_kernel, scale2),
        out_shape=out,
        in_specs=[pl.BlockSpec(memory_space=pl.ANY)] * 4,
        out_specs=vmem,
        scratch_shapes=[
            pltpu.VMEM((2, len(RELATIVE), SIDE, SIDE, 2, GROUP_ROWS, width), jnp.bfloat16),
            pltpu.VMEM((2, tokens_here, heads, width), jnp.bfloat16),
            pltpu.VMEM((2 * rows, width), jnp.bfloat16),
            pltpu.VMEM((2 * rows, 128), jnp.float32),
            pltpu.VMEM((2 * rows, 128), jnp.float32),
            pltpu.VMEM((2 * rows, width), jnp.float32),
            pltpu.VMEM((rows, width), jnp.bfloat16),
            pltpu.VMEM((rows, width), jnp.bfloat16),
            pltpu.VMEM((2 * rows // 128, 128), jnp.float32),
            pltpu.VMEM((2 * rows // 128, 128), jnp.float32),
            dma((4,)),
            dma((GROUPS, 2)),
            dma((GROUPS, 2)),
            dma((4, GROUPS)),
            dma((4, GROUPS)),
            dma((4, GROUPS)),
            dma((4, GROUPS)),
            dma((3,)),
            dma((3,)),
            dma((len(HOPS),)),
            dma((len(HOPS),)),
        ],
        compiler_params=pltpu.CompilerParams(
            collective_id=0, has_side_effects=True, vmem_limit_bytes=56 * 1024 * 1024
        ),
        cost_estimate=pl.CostEstimate(
            flops=4 * rows * 8192 * width, bytes_accessed=1 << 20, transcendentals=rows * 8192
        ),
    )(queries_first, queries_second, shared_keys, shared_values)
    return result[:, :heads], result[:, heads:]


def solution(mesh):
    return jax.shard_map(
        on_device,
        mesh=mesh,
        in_specs=(
            P("inner", "outer", None),
            P("inner", "outer", None),
            P(("inner", "outer"), None),
            P(("inner", "outer"), None),
        ),
        out_specs=(P("inner", "outer", None), P("inner", "outer", None)),
        check_vma=False,
    )
```
